128 devices in a mesh: seq: 8 (over z_hi, x), tensor: 16 (over z_lo, y, core).
Axes of the slice: x: 4, y: 4, z: 4 (z_hi: 2, z_lo: 2; z = z_hi * 2 + z_lo), core: 2. Of those that a mesh axis runs over, the one named last changes fastest.
Arguments:
- inputs: bfloat16 [3072, 4096], P('seq', 'tensor'), may hold values from -6 to 6
- w_gate: bfloat16 [4096, 14336], P(None, 'tensor'), may hold values from -0.125 to 0.125
- w_up: bfloat16 [4096, 14336], P(None, 'tensor'), may hold values from -0.125 to 0.125
- w_down: bfloat16 [14336, 4096], P('tensor'), may hold values from -0.046875 to 0.046875
- cotangents: float32 [4, 3072, 4096], P(None, 'seq', 'tensor'), may hold values from -3 to 3
- prefix_widths: int32 [4], replicated, may hold values from 128 to 14336, as said below
- block_rank: int32 [112], P('tensor'), may hold values from 0 to 111, each once
Outputs:
- input_grads: bfloat16 [3072, 4096], P('seq', 'tensor')
- grad_gate: bfloat16 [4096, 14336], P('seq', 'tensor')
- grad_up: bfloat16 [4096, 14336], P('seq', 'tensor')
- grad_down: bfloat16 [14336, 4096], P('tensor', 'seq')
The draws below stay inside these ranges and needn't reach their ends.
Inputs may be any that keep to these rules, and one draw needn't show every extreme that they name: prefix_widths[0] = 14336; the widths do not increase with g and are multiples of 128. `block_rank`: each number of 0 to 111 appears once.
All inputs are finite; a program needn't handle non-finite values.
Results may differ from the reference program's by a relative error of at most 0.025.
Values may be sent and summed in bfloat16 or wider, within the bound.
A program may use at most 192 MiB of HBM per device.

```python
import jax
import jax.numpy as jnp
from jax import lax

D = 4096
FF = 14336
BLOCK = 128
LEVELS = 4
TOK_DEV = 384
TOKENS = 3072
BLOCKS = 112
N_SEQ = 8


def draw_prefix_widths(key, part):
    key = jax.random.fold_in(key, 11)
    keys = jax.random.split(key, LEVELS)
    widths = [jnp.array(BLOCKS, jnp.int32)]
    for level in range(1, LEVELS):
        lower = max(1, BLOCKS * 3 // 2 ** (level + 2))
        upper = max(lower, BLOCKS * 5 // 2 ** (level + 2))
        widths.append(jax.random.randint(keys[level], (), lower, upper + 1, dtype=jnp.int32))
    return (jnp.stack(widths) * BLOCK).astype(jnp.int32)


def spiked(entries, stream_key, source, target, blocks, factor):
    owner, partner = [(jnp.arange(entries.shape[dim]) // (entries.shape[dim] // blocks)).reshape([-1 if axis == dim else 1 for axis in range(entries.ndim)]) for dim in (source, target)]
    chosen = jax.random.permutation(stream_key, blocks)[partner]
    strong = (owner == chosen) | (owner == (partner + blocks // 2) % blocks)
    return jnp.where(strong, factor * entries, entries)


def shard_levels(own_key, extent, cuts, least, largest):
    def one(axis_at, blocks):
        heights = jax.random.uniform(jax.random.fold_in(jax.random.fold_in(own_key, 6), axis_at), (blocks,), jnp.float32, least / len(cuts), largest / len(cuts))
        return jnp.repeat(jnp.exp(heights), extent[axis_at] // blocks).reshape((-1,) + (1,) * (len(extent) - axis_at - 1))

    level = one(*cuts[0])
    for cut in cuts[1:]:
        level = level * one(*cut)
    return level


def gaussian(key, extent, deviation, most, pieces=(), kind=jnp.bfloat16):
    loudness = shard_levels(key, extent, pieces, -0.22, 0.18) if pieces else 1.0
    values = jax.random.normal(key, extent, jnp.float32) * deviation * loudness
    return jnp.minimum(jnp.maximum(values, -most), most).astype(kind)


def gaussian_with(stream_key, extent, deviation, bound, cuts, heavy, kind=jnp.bfloat16):
    values = deviation * jax.random.normal(stream_key, extent, jnp.float32)
    if cuts:
        values = values * shard_levels(stream_key, extent, cuts, -0.22, 0.18)
    return jnp.clip(spiked(values, jax.random.fold_in(stream_key, 3), *heavy), -bound, bound).astype(kind)


def setup_inputs(seed: int = 0) -> dict:
    streams_of = jax.random.split(jax.random.key(seed), 8)
    return {
        "inputs": gaussian(streams_of[0], (TOKENS, D), 1.0, 6.0, ((0, 8), (1, 16))),
        "w_gate": gaussian_with(streams_of[1], (D, FF), D ** -0.5, 0.125, ((1, 16),), (1, 0, 16, 2.0)),
        "w_up": gaussian_with(streams_of[2], (D, FF), D ** -0.5, 0.125, ((1, 16),), (1, 0, 16, 2.0)),
        "w_down": gaussian(streams_of[3], (FF, D), FF ** -0.5, 0.046875, ((0, 16),)),
        "cotangents": gaussian(streams_of[4], (LEVELS, TOKENS, D), 0.5, 3.0, ((1, 8), (2, 16)), jnp.float32),
        "prefix_widths": draw_prefix_widths(jax.random.fold_in(streams_of[7], 71), 0),
        "block_rank": jax.random.permutation(streams_of[6], BLOCKS).astype(jnp.int32),
    }


def reference(inputs, w_gate, w_up, w_down, cotangents, prefix_widths, block_rank):
    gate = jnp.dot(inputs, w_gate, preferred_element_type=jnp.float32)
    up = jnp.dot(inputs, w_up, preferred_element_type=jnp.float32)
    sigma = jax.nn.sigmoid(gate)
    active = gate * sigma
    hidden = (active * up).astype(jnp.bfloat16)
    levels = jnp.sum((block_rank[:, None] * BLOCK < prefix_widths[None, :]).astype(jnp.int32), axis=1)
    level_sums = jnp.cumsum(cotangents.astype(jnp.float32), axis=0).astype(jnp.bfloat16)
    hidden_t = jnp.transpose(hidden.reshape(TOKENS, BLOCKS, BLOCK), (1, 0, 2))
    down_weight_blocks = w_down.reshape(BLOCKS, BLOCK, D)

    def block_share(items):
        hid_block, down_block, level = items
        selected_width = level_sums[level - 1]
        grad_block = jnp.dot(selected_width, down_block.T, preferred_element_type=jnp.float32)
        hid_runs = hid_block.reshape(N_SEQ, TOK_DEV, BLOCK).astype(jnp.float32)
        selected_passes = selected_width.reshape(N_SEQ, TOK_DEV, D).astype(jnp.float32)
        parts = jnp.einsum("sti,std->sid", hid_runs, selected_passes)
        rounded = lax.optimization_barrier(parts.astype(jnp.bfloat16))
        return grad_block, jnp.sum(rounded.astype(jnp.float32), axis=0)

    grad_blocks, down_parts = lax.map(block_share, (hidden_t, down_weight_blocks, levels))
    hidden_grad = jnp.transpose(grad_blocks, (1, 0, 2)).reshape(TOKENS, FF)
    grad_down = down_parts.reshape(FF, D).astype(jnp.bfloat16)
    gate_grad = (hidden_grad * up * sigma * (1.0 + gate * (1.0 - sigma))).astype(jnp.bfloat16)
    up_grad = (hidden_grad * active).astype(jnp.bfloat16)
    input_grads = (jnp.dot(gate_grad, w_gate.T, preferred_element_type=jnp.float32)
                   + jnp.dot(up_grad, w_up.T, preferred_element_type=jnp.float32)).astype(jnp.bfloat16)

    def accumulate(carry, items):
        rows, grad_g, grad_u = items
        part_g = lax.optimization_barrier(jnp.dot(rows.T, grad_g, preferred_element_type=jnp.float32).astype(jnp.bfloat16))
        part_u = lax.optimization_barrier(jnp.dot(rows.T, grad_u, preferred_element_type=jnp.float32).astype(jnp.bfloat16))
        return (carry[0] + part_g.astype(jnp.float32), carry[1] + part_u.astype(jnp.float32)), None

    start = (jnp.zeros((D, FF), jnp.float32), jnp.zeros((D, FF), jnp.float32))
    grand_sums, _ = lax.scan(accumulate, start, (inputs.reshape(N_SEQ, TOK_DEV, D),
                                             gate_grad.reshape(N_SEQ, TOK_DEV, FF),
                                             up_grad.reshape(N_SEQ, TOK_DEV, FF)))
    return input_grads, grand_sums[0].astype(jnp.bfloat16), grand_sums[1].astype(jnp.bfloat16), grad_down
```

```python
import functools

import jax
import jax.numpy as jnp
from jax import lax
from jax.experimental import pallas as pl
from jax.experimental.pallas import tpu as pltpu
from jax.sharding import PartitionSpec as P

BLOCK = 128
LEVELS = 4
MESH = pl.DeviceIdType.MESH
COPIES = 128
F32 = jnp.float32
BF16 = jnp.bfloat16
NT = (((1,), (1,)), ((), ()))
ORDER = ((0, 0), (1, 0), (0, 3), (0, 1), (1, 3), (1, 1), (0, 2), (1, 2))


def dot(a, b):
    return jnp.dot(a, b, preferred_element_type=F32)


def dot_nt(a, b):
    return lax.dot_general(a, b, NT, preferred_element_type=F32)


def cols(start, size):
    return pl.ds(pl.multiple_of(start, 128), size)


def rows(start, size):
    return pl.ds(pl.multiple_of(start, 16), size)


def body(tok, width, units, *refs):
    widths, rank, xin, wg, wu, wd, cot, o_in, o_g, o_u, o_d = refs[:11]
    (X, wt, wdb, wrow, XTs, XT, G, D, R1, R2, R3, Ps, Pr, IrC, IrZ, IrY, A, B, HG, hT,
     ss, rs, ls, s1, r1, s2, r2) = refs[11 + 8:]
    LS = {place: refs[11 + i] for i, place in enumerate(ORDER)}
    nb = units // BLOCK
    half_t = tok // 2
    half_u = units // 2
    nchunk = 2 * units // 256

    s, t = lax.axis_index("seq"), lax.axis_index("tensor")
    x, zh = lax.rem(s, 4), s // 4
    zl, y, c = t // 8, lax.rem(t // 2, 4), lax.rem(t, 2)
    at_x = lambda k: (zh * 4 + lax.rem(x + k, 4), t)
    at_y = lambda k: (s, zl * 8 + lax.rem(y + k, 4) * 2 + c)
    C = (s, t + 1 - 2 * c)
    Z1 = (s, t + 8 - 16 * zl)
    Z2 = ((1 - zh) * 4 + x, t)
    Xp, Xm, X2, Yp, Ym, Y2 = at_x(1), at_x(3), at_x(2), at_y(1), at_y(3), at_y(2)

    started = []
    local = []

    def send(src, dst, dev):
        i = len(started)
        cp = pltpu.make_async_remote_copy(
            src_ref=src, dst_ref=dst, send_sem=ss.at[i], recv_sem=rs.at[i],
            device_id=dev, device_id_type=MESH)
        cp.start()
        started.append(cp)
        return cp

    def load(src, dst):
        i = len(local)
        cp = pltpu.make_async_copy(src, dst, ls.at[i])
        cp.start()
        local.append(cp)
        return cp

    cot_loads = [load(cot.at[g], A.at[:, cols(256 * g, 256)]) for g in range(3)]
    cot_loads.append(load(cot.at[3], B.at[:, cols(0, 256)]))
    own_x = load(xin, X.at[:, cols(t * 256, 256)])

    def tile_loads(b, slot):
        return (
            pltpu.make_async_copy(wg.at[:, cols(b * BLOCK, BLOCK)], wt.at[slot, :, cols(0, BLOCK)],
                                  ls.at[16 + 2 * slot]),
            pltpu.make_async_copy(wu.at[:, cols(b * BLOCK, BLOCK)], wt.at[slot, :, cols(BLOCK, BLOCK)],
                                  ls.at[17 + 2 * slot]),
        )

    for slot in range(2):
        for cp in tile_loads(slot, slot):
            cp.start()

    def feature_slice(place):
        return (zl + place[0] - 2 * zl * place[0]) * 4 + lax.rem(y + place[1], 4)

    def down_load(k):
        return pltpu.make_async_copy(wd.at[:, cols(feature_slice(ORDER[k]) * 512, 512)],
                                     wdb.at[k % 2], ls.at[20 + k % 2])

    down_load(0).start()
    down_load(1).start()

    barrier = pltpu.get_barrier_semaphore()
    peers = (C, Z1, Z2, Xp, Xm, X2, Yp, Ym, Y2)
    for dev in peers:
        pl.semaphore_signal(barrier, inc=1, device_id=dev, device_id_type=MESH)
    pl.semaphore_wait(barrier, len(peers))

    def x_view(dz, dy, half):
        tt = (zl + dz - 2 * zl * dz) * 8 + lax.rem(y + dy, 4) * 2 + c
        if half is None:
            return X.at[:, cols(tt * 256, 256)]
        return X.at[pl.ds(half * half_t, half_t), cols(tt * 256, 256)]

    def ls_view(dz, dy, half):
        if half is None:
            return LS[(dz, dy)].at[c]
        return LS[(dz, dy)].at[c, pl.ds(half * 2, 2)]

    def x_pair(dz, dy, half, step):
        return x_view(dz, dy, half), x_view(dz, dy, half)

    def ls_pair(dz, dy, half, step):
        moved = {"C": (dz, dy), "Z": (1 - dz, dy), "P": (dz, (dy + 3) % 4), "M": (dz, (dy + 1) % 4)}[step]
        return ls_view(dz, dy, half), ls_view(moved[0], moved[1], half)

    where = {"C": C, "Z": Z1, "P": Yp, "M": Ym}

    def gather_send(pair, dz, dy, half, step, src=None):
        a, b = pair(dz, dy, half, step)
        return send(a if src is None else src, b, where[step])

    to_z = gather_send(x_pair, 0, 0, None, "Z", xin)
    to_p = {0: gather_send(x_pair, 0, 0, None, "P", xin)}
    to_m = {0: gather_send(x_pair, 0, 0, None, "M", xin)}
    to_c = [gather_send(x_pair, 0, 0, None, "C", xin)]

    for cp in cot_loads:
        cp.wait()
    total = A[:, 0:256]
    own = LS[(0, 0)]
    own[c, 0] = total.astype(BF16)
    for g in range(1, LEVELS):
        total = total + (A[:, 256 * g:256 * g + 256] if g < 3 else B[:, 0:256])
        own[c, g] = total.astype(BF16)

    to_z.wait_recv()
    to_p[1] = gather_send(x_pair, 1, 0, None, "P")
    to_m[1] = gather_send(x_pair, 1, 0, None, "M")
    to_c.append(gather_send(x_pair, 1, 0, None, "C"))
    l_to_z = gather_send(ls_pair, 0, 0, None, "Z")
    l_to_c = {(0, 0): gather_send(ls_pair, 0, 0, None, "C")}
    opp = {}
    for dz in range(2):
        to_p[dz].wait_recv()
        opp[dz, 0] = gather_send(x_pair, dz, 3, 0, "P")
        to_c.append(gather_send(x_pair, dz, 3, None, "C"))
        to_m[dz].wait_recv()
        opp[dz, 1] = gather_send(x_pair, dz, 1, 1, "M")
        to_c.append(gather_send(x_pair, dz, 1, None, "C"))
    l_to_p = {0: gather_send(ls_pair, 0, 0, None, "P")}
    l_to_m = {0: gather_send(ls_pair, 0, 0, None, "M")}
    for dz in range(2):
        opp[dz, 0].wait_recv()
        opp[dz, 1].wait_recv()
        to_c.append(gather_send(x_pair, dz, 2, None, "C"))
    own_x.wait()
    for cp in to_c:
        cp.wait_recv()

    x_sends = [to_z, *to_p.values(), *to_m.values(), *opp.values(), *to_c]

    def transposed(k):
        return jnp.transpose(X[:, cols((c * 4 + lax.rem(x + k, 4)) * 512, 512)])

    x_moves = []
    for k, dev in ((1, Xp), (3, Xm), (2, X2)):
        XTs[k - 1] = transposed(k)
        x_moves.append((4 - k, send(XTs.at[k - 1], XT.at[c, :, cols((4 - k) * tok, tok)], dev)))
    XT[c, :, 0:tok] = transposed(0)
    xt_c = [send(XT.at[c, :, cols(0, tok)], XT.at[c, :, cols(0, tok)], C)]

    def forward(b, _):
        slot = lax.rem(b, 2)
        for cp in tile_loads(b, slot):
            cp.wait()
        both = dot(X[...], wt[slot])

        @pl.when(b + 2 < nb)
        def _():
            for cp in tile_loads(b + 2, slot):
                cp.start()

        gate, up = both[:, :BLOCK], both[:, BLOCK:]
        sigma = jax.nn.sigmoid(gate)
        active = gate * sigma
        at = cols(b * BLOCK, BLOCK)
        A[:, at] = up * sigma * (1.0 + gate * (1.0 - sigma))
        B[:, at] = active
        hT[rows(b * BLOCK, BLOCK), :] = jnp.transpose((active * up).astype(BF16))
        return 0

    lax.fori_loop(0, nb, forward, 0)

    for k, cp in x_moves:
        cp.wait_recv()
        piece = XT.at[c, :, cols(k * tok, tok)]
        xt_c.append(send(piece, piece, C))

    def relation(place):
        return lax.rem(y + place[1] - x + 4, 4)

    def owner_z(place):
        return zl + place[0] - 2 * zl * place[0]

    def reduce_copy(place, kind):
        dz, dy = place
        zz = owner_z(place)
        if kind < 2:
            return pltpu.make_async_remote_copy(
                src_ref=D.at[dz, dy, pl.ds(kind * half_u, half_u)], dst_ref=R1.at[zz, kind],
                send_sem=s1.at[zz, kind], recv_sem=r1.at[zz, kind],
                device_id=Xp if kind == 0 else Xm, device_id_type=MESH)
        rel = relation(place)
        side = rel // 2
        h = 1 - side if kind == 2 else side
        span = rows(h * half_u, half_u)
        return pltpu.make_async_remote_copy(
            src_ref=D.at[dz, dy, span], dst_ref=R2.at[zz, side, span],
            send_sem=s2.at[zz, side, kind - 2], recv_sem=r2.at[zz, side, kind - 2],
            device_id=at_x(rel), device_id_type=MESH)

    def slice_work(k):
        place = ORDER[k]
        dz, dy = place
        src = LS[place]
        down_load(k).wait()

        def step(b, _):
            used = sum((rank[b] * BLOCK < widths[g]).astype(jnp.int32) for g in range(LEVELS))
            level = jnp.maximum(used - 1, 0)
            l0, l1 = src[0, level], src[1, level]
            at = rows(b * BLOCK, BLOCK)
            h = hT[at, :]
            D[dz, dy, at, 0:256] = dot(h, l0).astype(BF16)
            D[dz, dy, at, 256:512] = dot(h, l1).astype(BF16)
            part = dot_nt(l0, wdb[k % 2, at, 0:256]) + dot_nt(l1, wdb[k % 2, at, 256:512])
            lane = cols(b * BLOCK, BLOCK)
            HG[:, lane] = part if k == 0 else HG[:, lane] + part
            return 0

        lax.fori_loop(0, nb, step, 0)
        if k + 2 < len(ORDER):
            down_load(k + 2).start()
        rel = relation(place)

        @pl.when(rel == 2)
        def _():
            reduce_copy(place, 0).start()
            reduce_copy(place, 1).start()

        @pl.when(lax.rem(rel, 2) == 1)
        def _():
            reduce_copy(place, 2).start()

    def relay(k):
        place = ORDER[k]
        dz, dy = place
        rel = relation(place)
        zz = owner_z(place)
        side = rel // 2

        @pl.when(lax.rem(rel, 2) == 1)
        def _():
            pltpu.make_async_remote_copy(
                src_ref=D.at[dz, dy, pl.ds(0, half_u)], dst_ref=R1.at[zz, side],
                send_sem=s1.at[zz, side], recv_sem=r1.at[zz, side],
                device_id=Xp, device_id_type=MESH).wait_recv()
            span = rows(side * half_u, half_u)
            D[dz, dy, span, :] = (D[dz, dy, span, :].astype(F32) + R1[zz, side].astype(F32)).astype(BF16)
            reduce_copy(place, 3).start()

    l_to_z.wait_recv()
    l_to_p[1] = gather_send(ls_pair, 1, 0, None, "P")
    l_to_m[1] = gather_send(ls_pair, 1, 0, None, "M")
    l_to_c[1, 0] = gather_send(ls_pair, 1, 0, None, "C")
    l_to_c[0, 0].wait_recv()
    slice_work(0)
    l_to_c[1, 0].wait_recv()
    slice_work(1)
    l_opp = {}
    for dz in range(2):
        l_to_p[dz].wait_recv()
        l_opp[dz, 0] = gather_send(ls_pair, dz, 3, 0, "P")
        l_to_c[dz, 3] = gather_send(ls_pair, dz, 3, None, "C")
        l_to_m[dz].wait_recv()
        l_opp[dz, 1] = gather_send(ls_pair, dz, 1, 1, "M")
        l_to_c[dz, 1] = gather_send(ls_pair, dz, 1, None, "C")
        for i, dy in enumerate((3, 1)):
            l_to_c[dz, dy].wait_recv()
            slice_work(2 + 2 * dz + i)
    for dz in range(2):
        l_opp[dz, 0].wait_recv()
        l_opp[dz, 1].wait_recv()
        l_to_c[dz, 2] = gather_send(ls_pair, dz, 2, None, "C")
        l_to_c[dz, 2].wait_recv()
        slice_work(6 + dz)
    for k in range(len(ORDER)):
        relay(k)

    def grads(b, _):
        at = cols(b * BLOCK, BLOCK)
        hg = HG[:, at]
        G[0:tok, at] = (hg * A[:, at]).astype(BF16)
        G[0:tok, cols(units + b * BLOCK, BLOCK)] = (hg * B[:, at]).astype(BF16)
        return 0

    lax.fori_loop(0, nb, grads, 0)

    from_m, from_p, far = {}, {}, {}

    def g_own(j):
        at = cols(j * 256, 256)
        src = G.at[pl.ds(0, tok), at]
        from_m[j] = send(src, G.at[pl.ds(3 * tok, tok), at], Xp)
        from_p[j] = send(src, G.at[pl.ds(tok, tok), at], Xm)

    def g_forward(j):
        at = cols(j * 256, 256)
        from_m[j].wait_recv()
        far[j, 0] = send(G.at[pl.ds(3 * tok, half_t), at], G.at[pl.ds(2 * tok, half_t), at], Xp)
        from_p[j].wait_recv()
        far[j, 1] = send(G.at[pl.ds(tok + half_t, half_t), at],
                         G.at[pl.ds(2 * tok + half_t, half_t), at], Xm)

    p_sent = {}

    def p_other(j):
        far[j, 0].wait_recv()
        far[j, 1].wait_recv()
        at = cols(j * 256, 256)
        for h in range(2):
            Ps[j, pl.ds(256 * h, 256), :] = dot(XT[1 - zh, pl.ds(256 * h, 256), :], G[:, at]).astype(BF16)
        p_sent[j] = send(Ps.at[j], Pr.at[j], Z2)

    def p_own(j):
        p_sent[j].wait_recv()
        at = cols(j * 256, 256)
        for h in range(2):
            r = pl.ds(256 * h, 256)
            out = (dot(XT[zh, r, :], G[:, at]) + Pr[j, r, :].astype(F32)).astype(BF16)
            for i in range(2):
                lane = j * 256 + i * BLOCK
                target, lane = (o_g, lane) if lane < units else (o_u, lane - units)
                target[r, lane:lane + BLOCK] = out[:, i * BLOCK:(i + 1) * BLOCK]

    def row_loads(i, slot, core):
        at = rows((2 * i + core) * 256, 256)
        return (
            pltpu.make_async_copy(wg.at[at, :], wrow.at[slot, :, cols(0, units)], ls.at[16 + 2 * slot]),
            pltpu.make_async_copy(wu.at[at, :], wrow.at[slot, :, cols(units, units)], ls.at[17 + 2 * slot]),
        )

    def input_part(core, offset):
        def step(i, _):
            slot = lax.rem(i, 2)
            for cp in row_loads(i, slot, core):
                cp.wait()
            X[:, cols(offset + i * 256, 256)] = dot_nt(G[0:tok, :], wrow[slot]).astype(BF16)

            @pl.when(i + 2 < 8)
            def _():
                for cp in row_loads(i + 2, slot, core):
                    cp.start()
            return 0

        for slot in range(2):
            for cp in row_loads(slot, slot, core):
                cp.start()
        lax.fori_loop(0, 8, step, 0)

    g_own(0)
    g_own(1)
    for cp in x_sends:
        cp.wait_send()
    input_part(1 - c, 0)
    in_c = send(X.at[:, cols(0, 2048)], IrC.at[...], C)
    g_own(2)
    g_forward(0)
    input_part(c, 2048)
    g_own(3)
    g_forward(1)
    for cp in xt_c:
        cp.wait_recv()
    p_other(0)
    in_c.wait_recv()
    away = cols(2048 + (1 - zl) * 1024, 1024)
    X[:, away] = (X[:, away].astype(F32) + IrC[:, cols((1 - zl) * 1024, 1024)].astype(F32)).astype(BF16)
    in_z = send(X.at[:, away], IrZ.at[...], Z1)
    g_own(4)
    g_forward(2)
    p_other(1)
    p_own(0)

    def sum_x(zz):
        for side in range(2):
            for i in range(2):
                span = pl.ds(0, half_u)
                pltpu.make_async_remote_copy(
                    src_ref=D.at[0, 0, span], dst_ref=R2.at[zz, side, span],
                    send_sem=s2.at[zz, side, i], recv_sem=r2.at[zz, side, i],
                    device_id=Xp, device_id_type=MESH).wait_recv()
        dz = zl + zz - 2 * zl * zz
        dy = lax.rem(x - y + 4, 4)
        return dz, dy

    def down_away():
        zz = 1 - zh
        dz, dy = sum_x(zz)

        def step(b, _):
            at = rows(b * BLOCK, BLOCK)
            D[dz, dy, at, :] = (D[dz, dy, at, :].astype(F32) + R2[zz, 0, at, :].astype(F32)
                                + R2[zz, 1, at, :].astype(F32)).astype(BF16)
            return 0

        lax.fori_loop(0, nb, step, 0)
        return send(D.at[dz, dy], R3.at[...], Z2)

    def down_own(cp):
        zz = zh
        dz, dy = sum_x(zz)
        cp.wait_recv()

        def step(b, _):
            at = rows(b * BLOCK, BLOCK)
            o_d[at, :] = (D[dz, dy, at, :].astype(F32) + R2[zz, 0, at, :].astype(F32)
                          + R2[zz, 1, at, :].astype(F32) + R3[at, :].astype(F32)).astype(BF16)
            return 0

        lax.fori_loop(0, nb, step, 0)

    down_z = down_away()
    g_own(5)
    g_forward(3)
    p_other(2)
    p_own(1)
    in_z.wait_recv()
    kept = cols(2048 + zl * 1024, 1024)
    X[:, kept] = (X[:, kept].astype(F32) + IrC[:, cols(zl * 1024, 1024)].astype(F32)
                  + IrZ[...].astype(F32)).astype(BF16)
    in_y = []
    for k, dev in ((1, Yp), (3, Ym), (2, Y2)):
        src = X.at[:, cols(2048 + zl * 1024 + lax.rem(y + k, 4) * 256, 256)]
        in_y.append(send(src, IrY.at[k - 1], dev))
    g_own(6)
    g_forward(4)
    p_other(3)
    p_own(2)
    g_forward(5)
    p_other(4)
    p_own(3)
    for cp in in_y:
        cp.wait_recv()
    mine = X[:, cols(2048 + zl * 1024 + y * 256, 256)].astype(F32)
    for k in range(3):
        mine = mine + IrY[k].astype(F32)
    o_in[...] = mine.astype(BF16)
    g_forward(6)
    p_other(5)
    p_own(4)
    p_other(6)
    down_own(down_z)
    p_own(5)
    p_own(6)

    for cp in started:
        if not any(cp is other for other in x_sends):
            cp.wait_send()
    for place in ORDER:
        rel = relation(place)

        @pl.when(rel == 2)
        def _():
            reduce_copy(place, 0).wait_send()
            reduce_copy(place, 1).wait_send()

        @pl.when(lax.rem(rel, 2) == 1)
        def _():
            reduce_copy(place, 2).wait_send()
            reduce_copy(place, 3).wait_send()


def on_device(inputs, w_gate, w_up, w_down, cotangents, prefix_widths, block_rank):
    tok = inputs.shape[0]
    width, units = w_gate.shape
    anywhere = pl.BlockSpec(memory_space=pl.ANY)
    smem = pl.BlockSpec(memory_space=pltpu.SMEM)
    vmem = pl.BlockSpec(memory_space=pltpu.VMEM)
    share = width // 8
    V = pltpu.VMEM
    dma = pltpu.SemaphoreType.DMA
    scratch = [V((2, LEVELS, tok, 256), BF16) for _ in ORDER] + [
        V((tok, width), BF16),
        V((2, width, 256), BF16),
        V((2, units, 512), BF16),
        V((2, 256, 2 * units), BF16),
        V((3, 512, tok), BF16),
        V((2, 512, 4 * tok), BF16),
        V((4 * tok, 2 * units), BF16),
        V((2, 4, units, 512), BF16),
        V((2, 2, units // 2, 512), BF16),
        V((2, 2, units, 512), BF16),
        V((units, 512), BF16),
        V((7, 512, 256), BF16),
        V((7, 512, 256), BF16),
        V((tok, width // 2), BF16),
        V((tok, width // 4), BF16),
        V((3, tok, 256), BF16),
        V((tok, units), F32),
        V((tok, units), F32),
        V((tok, units), F32),
        V((units, tok), BF16),
        dma((COPIES,)),
        dma((COPIES,)),
        dma((24,)),
        dma((2, 2)),
        dma((2, 2)),
        dma((2, 2, 2)),
        dma((2, 2, 2)),
    ]
    return pl.pallas_call(
        functools.partial(body, tok, width, units),
        out_shape=(
            jax.ShapeDtypeStruct((tok, 256), BF16),
            jax.ShapeDtypeStruct((share, units), BF16),
            jax.ShapeDtypeStruct((share, units), BF16),
            jax.ShapeDtypeStruct((units, share), BF16),
        ),
        in_specs=[smem, smem] + [anywhere] * 5,
        out_specs=(vmem,) * 4,
        scratch_shapes=scratch,
        compiler_params=pltpu.CompilerParams(
            collective_id=0, has_side_effects=True, vmem_limit_bytes=64 * 2**20),
        name="swiglu_backward",
    )(prefix_widths, block_rank, inputs, w_gate, w_up, w_down, cotangents)


def solution(mesh):
    placed = (
        P("seq", "tensor"),
        P(None, "tensor"),
        P(None, "tensor"),
        P("tensor", None),
        P(None, "seq", "tensor"),
        P(),
        P("tensor"),
    )
    return jax.shard_map(
        on_device,
        mesh=mesh,
        in_specs=placed,
        out_specs=(P("seq", "tensor"), P("seq", "tensor"), P("seq", "tensor"), P("tensor", "seq")),
        check_vma=False,
    )
```

```python
import functools

import jax
import jax.numpy as jnp
from jax import lax
from jax.experimental import pallas as pl
from jax.experimental.pallas import tpu as pltpu
from jax.sharding import PartitionSpec as P

BLOCK = 128
LEVELS = 4
MESH = pl.DeviceIdType.MESH
COPIES = 128
F32 = jnp.float32
BF16 = jnp.bfloat16
NT = (((1,), (1,)), ((), ()))
ORDER = ((0, 0), (1, 0), (0, 3), (0, 1), (0, 2), (1, 3), (1, 1), (1, 2))


def dot(a, b):
    return jnp.dot(a, b, preferred_element_type=F32)


def dot_nt(a, b):
    return lax.dot_general(a, b, NT, preferred_element_type=F32)


def cols(start, size):
    return pl.ds(pl.multiple_of(start, 128), size)


def rows(start, size):
    return pl.ds(pl.multiple_of(start, 16), size)


def body(tok, width, units, *refs):
    widths, rank, xin, wg, wu, wd, cot, o_in, o_g, o_u, o_d = refs[:11]
    (X, wt, wdb, wrow, XTs, XT, G, D, R1, R2, R3, Ps, Pr, IrC, IrZ, IrY, A, B, HG, hT,
     ss, rs, ls, s1, r1, s2, r2) = refs[11 + 8:]
    LS = {place: refs[11 + i] for i, place in enumerate(ORDER)}
    nb = units // BLOCK
    half_t, quarter = tok // 2, tok // 4
    half_u = units // 2
    nchunk = 2 * units // 256

    s, t = lax.axis_index("seq"), lax.axis_index("tensor")
    x, zh = lax.rem(s, 4), s // 4
    zl, y, c = t // 8, lax.rem(t // 2, 4), lax.rem(t, 2)
    at_x = lambda k: (zh * 4 + lax.rem(x + k, 4), t)
    at_y = lambda k: (s, zl * 8 + lax.rem(y + k, 4) * 2 + c)
    C = (s, t + 1 - 2 * c)
    Z1 = (s, t + 8 - 16 * zl)
    Z2 = ((1 - zh) * 4 + x, t)
    Xp, Xm, X2, Yp, Ym, Y2 = at_x(1), at_x(3), at_x(2), at_y(1), at_y(3), at_y(2)

    started = []
    local = []

    def send(src, dst, dev):
        i = len(started)
        cp = pltpu.make_async_remote_copy(
            src_ref=src, dst_ref=dst, send_sem=ss.at[i], recv_sem=rs.at[i],
            device_id=dev, device_id_type=MESH)
        cp.start()
        started.append(cp)
        return cp

    def load(src, dst):
        i = len(local)
        cp = pltpu.make_async_copy(src, dst, ls.at[i])
        cp.start()
        local.append(cp)
        return cp

    cot_loads = [load(cot.at[g], A.at[:, cols(256 * g, 256)]) for g in range(3)]
    cot_loads.append(load(cot.at[3], B.at[:, cols(0, 256)]))
    own_x = load(xin, X.at[:, cols(t * 256, 256)])

    half_w = width // 2

    def tile_half(n):
        h = n // nb
        return zl + h - 2 * zl * h

    def tile_loads(n, slot):
        at, lane = rows(tile_half(n) * half_w, half_w), cols(lax.rem(n, nb) * BLOCK, BLOCK)
        return (
            pltpu.make_async_copy(wg.at[at, lane], wt.at[slot, :, cols(0, BLOCK)], ls.at[8 + 2 * slot]),
            pltpu.make_async_copy(wu.at[at, lane], wt.at[slot, :, cols(BLOCK, BLOCK)], ls.at[9 + 2 * slot]),
        )

    for slot in range(4):
        for cp in tile_loads(slot, slot):
            cp.start()

    def feature_slice(place):
        return (zl + place[0] - 2 * zl * place[0]) * 4 + lax.rem(y + place[1], 4)

    def down_load(k):
        return pltpu.make_async_copy(wd.at[:, cols(feature_slice(ORDER[k]) * 512, 512)],
                                     wdb.at[k % 2], ls.at[20 + k % 2])

    down_load(0).start()
    down_load(1).start()

    barrier = pltpu.get_barrier_semaphore()
    peers = (C, Z1, Z2, Xp, Xm, X2, Yp, Ym, Y2)
    for dev in peers:
        pl.semaphore_signal(barrier, inc=1, device_id=dev, device_id_type=MESH)
    pl.semaphore_wait(barrier, len(peers))

    def x_view(place, first, count):
        tt = feature_slice(place) * 2 + c
        return X.at[pl.ds(first * quarter, count * quarter), cols(tt * 256, 256)]

    def x_pair(place, moved, first, count):
        return x_view(place, first, count), x_view(place, first, count)

    def ls_pair(place, moved, first, count):
        levels = pl.ds(first, count)
        return LS[place].at[c, levels], LS[moved].at[c, levels]

    class Gather:
        def __init__(self, pair, cut):
            self.pair = pair
            self.cut = cut
            self.moves = {}

        def send(self, step, place, first=0, count=4, src=None):
            dz, dy = place
            moved, dev = {"C": (place, C), "Z": ((1 - dz, dy), Z1), "P": ((dz, (dy + 3) % 4), Yp),
                          "M": ((dz, (dy + 1) % 4), Ym)}[step]
            mine, there = self.pair(place, moved, first, count)
            self.moves[step, place] = send(mine if src is None else src, there, dev)

        def got(self, step, place):
            self.moves[step, place].wait_recv()

        def late_z(self, place):
            if self.cut < 4:
                self.send("Z", place, self.cut, 4 - self.cut)

        def got_late_z(self, place):
            if self.cut < 4:
                self.got("Z", place)

        def along_z(self):
            self.got("Z", (0, 0))
            self.send("P", (1, 0), 0, self.cut)
            self.send("M", (1, 0), 0, self.cut)
            self.send("C", (1, 0))

        def neighbours0(self):
            self.got("P", (0, 0))
            self.send("P", (0, 3), 0, 2)
            self.late_z((0, 3))
            self.send("C", (0, 3))
            self.got("M", (0, 0))
            self.send("M", (0, 1), 2, 2)
            self.late_z((0, 1))
            self.send("C", (0, 1))

        def opposite0(self):
            self.got("P", (0, 3))
            self.got("M", (0, 1))
            self.late_z((0, 2))
            self.send("C", (0, 2))

        def neighbours1(self):
            self.got("P", (1, 0))
            self.send("P", (1, 3), 0, self.cut // 2)
            self.got("M", (1, 0))
            self.send("M", (1, 1), self.cut // 2, self.cut // 2)
            self.got_late_z((0, 3))
            self.send("C", (1, 3))
            self.got_late_z((0, 1))
            self.send("C", (1, 1))

        def opposite1(self):
            self.got("P", (1, 3))
            self.got("M", (1, 1))
            self.got_late_z((0, 2))
            self.send("C", (1, 2))

    gx, gl = Gather(x_pair, 4), Gather(ls_pair, 2)
    for step in "ZPMC":
        gx.send(step, (0, 0), src=xin)

    for cp in cot_loads:
        cp.wait()
    total = A[:, 0:256]
    own = LS[(0, 0)]
    own[c, 0] = total.astype(BF16)
    for g in range(1, LEVELS):
        total = total + (A[:, 256 * g:256 * g + 256] if g < 3 else B[:, 0:256])
        own[c, g] = total.astype(BF16)

    gx.along_z()
    gl.send("Z", (0, 0))
    gl.send("C", (0, 0))
    gx.neighbours0()
    gx.opposite0()
    gx.neighbours1()
    gl.send("P", (0, 0))
    gl.send("M", (0, 0))
    own_x.wait()
    for dy in range(4):
        gx.got("C", (0, dy))

    def forward_part(n):
        slot = lax.rem(n, 4)
        for cp in tile_loads(n, slot):
            cp.wait()
        return dot(X[:, cols(tile_half(n) * half_w, half_w)], wt[slot])

    def tile_next(n):
        @pl.when(n + 4 < 2 * nb)
        def _():
            for cp in tile_loads(n + 4, lax.rem(n, 4)):
                cp.start()

    def forward_first(b, _):
        both = forward_part(b)
        tile_next(b)
        at = cols(b * BLOCK, BLOCK)
        A[:, at] = both[:, :BLOCK]
        B[:, at] = both[:, BLOCK:]
        return 0

    def forward(b, _):
        both = forward_part(b + nb)
        tile_next(b + nb)
        at = cols(b * BLOCK, BLOCK)
        gate, up = both[:, :BLOCK] + A[:, at], both[:, BLOCK:] + B[:, at]
        sigma = jax.nn.sigmoid(gate)
        active = gate * sigma
        A[:, at] = up * sigma * (1.0 + gate * (1.0 - sigma))
        B[:, at] = active
        hT[rows(b * BLOCK, BLOCK), :] = jnp.transpose((active * up).astype(BF16))
        return 0

    lax.fori_loop(0, nb, forward_first, 0)
    gx.opposite1()
    for dy in range(4):
        gx.got("C", (1, dy))
    x_sends = list(gx.moves.values())

    def transposed(k):
        return jnp.transpose(X[:, cols((c * 4 + lax.rem(x + k, 4)) * 512, 512)])

    x_moves = []
    for k, dev in ((1, Xp), (3, Xm), (2, X2)):
        XTs[k - 1] = transposed(k)
        x_moves.append((4 - k, send(XTs.at[k - 1], XT.at[c, :, cols((4 - k) * tok, tok)], dev)))
    XT[c, :, 0:tok] = transposed(0)
    xt_c = [send(XT.at[c, :, cols(0, tok)], XT.at[c, :, cols(0, tok)], C)]

    lax.fori_loop(0, nb, forward, 0)

    def relation(place):
        return lax.rem(y + place[1] - x + 4, 4)

    def owner_z(place):
        return zl + place[0] - 2 * zl * place[0]

    def reduce_copy(place, kind):
        dz, dy = place
        zz = owner_z(place)
        if kind < 2:
            return pltpu.make_async_remote_copy(
                src_ref=D.at[dz, dy, pl.ds(kind * half_u, half_u)], dst_ref=R1.at[zz, kind],
                send_sem=s1.at[zz, kind], recv_sem=r1.at[zz, kind],
                device_id=Xp if kind == 0 else Xm, device_id_type=MESH)
        rel = relation(place)
        side = rel // 2
        h = 1 - side if kind == 2 else side
        span = rows(h * half_u, half_u)
        return pltpu.make_async_remote_copy(
            src_ref=D.at[dz, dy, span], dst_ref=R2.at[zz, side, span],
            send_sem=s2.at[zz, side, kind - 2], recv_sem=r2.at[zz, side, kind - 2],
            device_id=at_x(rel), device_id_type=MESH)

    def slice_work(k):
        place = ORDER[k]
        dz, dy = place
        src = LS[place]
        down_load(k).wait()

        def step(b, _):
            used = sum((rank[b] * BLOCK < widths[g]).astype(jnp.int32) for g in range(LEVELS))
            level = jnp.maximum(used - 1, 0)
            l0, l1 = src[0, level], src[1, level]
            at = rows(b * BLOCK, BLOCK)
            h = hT[at, :]
            D[dz, dy, at, 0:256] = dot(h, l0).astype(BF16)
            D[dz, dy, at, 256:512] = dot(h, l1).astype(BF16)
            part = dot_nt(l0, wdb[k % 2, at, 0:256]) + dot_nt(l1, wdb[k % 2, at, 256:512])
            lane = cols(b * BLOCK, BLOCK)
            HG[:, lane] = part if k == 0 else HG[:, lane] + part
            return 0

        lax.fori_loop(0, nb, step, 0)
        if k + 2 < len(ORDER):
            down_load(k + 2).start()
        rel = relation(place)

        @pl.when(rel == 2)
        def _():
            reduce_copy(place, 0).start()
            reduce_copy(place, 1).start()

        @pl.when(lax.rem(rel, 2) == 1)
        def _():
            reduce_copy(place, 2).start()

    def relay(k):
        place = ORDER[k]
        dz, dy = place
        rel = relation(place)
        zz = owner_z(place)
        side = rel // 2

        @pl.when(lax.rem(rel, 2) == 1)
        def _():
            pltpu.make_async_remote_copy(
                src_ref=D.at[dz, dy, pl.ds(0, half_u)], dst_ref=R1.at[zz, side],
                send_sem=s1.at[zz, side], recv_sem=r1.at[zz, side],
                device_id=Xp, device_id_type=MESH).wait_recv()
            span = rows(side * half_u, half_u)
            D[dz, dy, span, :] = (D[dz, dy, span, :].astype(F32) + R1[zz, side].astype(F32)).astype(BF16)
            reduce_copy(place, 3).start()

    gl.along_z()
    gl.got("C", (0, 0))
    slice_work(0)
    gl.neighbours0()
    gl.got("C", (1, 0))
    slice_work(1)
    gl.got("C", (0, 3))
    slice_work(2)
    gl.got("C", (0, 1))
    slice_work(3)
    gl.opposite0()
    for k, cp in x_moves:
        cp.wait_recv()
        piece = XT.at[c, :, cols(k * tok, tok)]
        xt_c.append(send(piece, piece, C))
    relay(0)
    gl.got("C", (0, 2))
    slice_work(4)
    gl.neighbours1()
    relay(1)
    gl.got("C", (1, 3))
    slice_work(5)
    gl.got("C", (1, 1))
    slice_work(6)
    gl.opposite1()
    relay(2)
    relay(3)
    gl.got("C", (1, 2))
    slice_work(7)
    relay(4)

    def grads(b, _):
        at = cols(b * BLOCK, BLOCK)
        hg = HG[:, at]
        G[0:tok, at] = (hg * A[:, at]).astype(BF16)
        G[0:tok, cols(units + b * BLOCK, BLOCK)] = (hg * B[:, at]).astype(BF16)
        return 0

    lax.fori_loop(0, nb, grads, 0)

    from_m, from_p, far = {}, {}, {}

    def g_own(j):
        at = cols(j * 256, 256)
        src = G.at[pl.ds(0, tok), at]
        from_m[j] = send(src, G.at[pl.ds(3 * tok, tok), at], Xp)
        from_p[j] = send(src, G.at[pl.ds(tok, tok), at], Xm)

    def g_forward(j):
        at = cols(j * 256, 256)
        from_m[j].wait_recv()
        far[j, 0] = send(G.at[pl.ds(3 * tok, half_t), at], G.at[pl.ds(2 * tok, half_t), at], Xp)
        from_p[j].wait_recv()
        far[j, 1] = send(G.at[pl.ds(tok + half_t, half_t), at],
                         G.at[pl.ds(2 * tok + half_t, half_t), at], Xm)

    p_sent = {}

    def p_other(j):
        far[j, 0].wait_recv()
        far[j, 1].wait_recv()
        at = cols(j * 256, 256)
        for h in range(2):
            Ps[j, pl.ds(256 * h, 256), :] = dot(XT[1 - zh, pl.ds(256 * h, 256), :], G[:, at]).astype(BF16)
        p_sent[j] = send(Ps.at[j], Pr.at[j], Z2)

    def p_own(j):
        p_sent[j].wait_recv()
        at = cols(j * 256, 256)
        for h in range(2):
            r = pl.ds(256 * h, 256)
            out = (dot(XT[zh, r, :], G[:, at]) + Pr[j, r, :].astype(F32)).astype(BF16)
            for i in range(2):
                lane = j * 256 + i * BLOCK
                target, lane = (o_g, lane) if lane < units else (o_u, lane - units)
                target[r, lane:lane + BLOCK] = out[:, i * BLOCK:(i + 1) * BLOCK]

    def row_loads(i, slot, core):
        at = rows((2 * i + core) * 256, 256)
        return (
            pltpu.make_async_copy(wg.at[at, :], wrow.at[slot, :, cols(0, units)], ls.at[16 + 2 * slot]),
            pltpu.make_async_copy(wu.at[at, :], wrow.at[slot, :, cols(units, units)], ls.at[17 + 2 * slot]),
        )

    def input_part(core, offset):
        def step(i, _):
            slot = lax.rem(i, 2)
            for cp in row_loads(i, slot, core):
                cp.wait()
            X[:, cols(offset + i * 256, 256)] = dot_nt(G[0:tok, :], wrow[slot]).astype(BF16)

            @pl.when(i + 2 < 8)
            def _():
                for cp in row_loads(i + 2, slot, core):
                    cp.start()
            return 0

        for slot in range(2):
            for cp in row_loads(slot, slot, core):
                cp.start()
        lax.fori_loop(0, 8, step, 0)

    def sum_x(zz):
        for side in range(2):
            for i in range(2):
                span = pl.ds(0, half_u)
                pltpu.make_async_remote_copy(
                    src_ref=D.at[0, 0, span], dst_ref=R2.at[zz, side, span],
                    send_sem=s2.at[zz, side, i], recv_sem=r2.at[zz, side, i],
                    device_id=Xp, device_id_type=MESH).wait_recv()
        return down_place(zz)

    def down_place(zz):
        return zl + zz - 2 * zl * zz, lax.rem(x - y + 4, 4)

    down_z = []

    def down_away(half):
        zz = 1 - zh
        dz, dy = sum_x(zz) if half == 0 else down_place(zz)
        at = pl.ds(half * half_u, half_u)
        D[dz, dy, at, :] = (D[dz, dy, at, :].astype(F32) + R2[zz, 0, at, :].astype(F32)
                            + R2[zz, 1, at, :].astype(F32)).astype(BF16)
        down_z.append(send(D.at[dz, dy, at], R3.at[at], Z2))

    def down_own():
        zz = zh
        dz, dy = sum_x(zz)
        for cp in down_z:
            cp.wait_recv()

        def step(b, _):
            at = rows(b * BLOCK, BLOCK)
            o_d[at, :] = (D[dz, dy, at, :].astype(F32) + R2[zz, 0, at, :].astype(F32)
                          + R2[zz, 1, at, :].astype(F32) + R3[at, :].astype(F32)).astype(BF16)
            return 0

        lax.fori_loop(0, nb, step, 0)

    in_y, in_z = [], []

    def input_sum_cores():
        in_c.wait_recv()
        for i in range(8):
            at = cols(2048 + 256 * i, 256)
            X[:, at] = (X[:, at].astype(F32) + IrC[:, cols(256 * i, 256)].astype(F32)).astype(BF16)
        for k, dev in ((1, Yp), (3, Ym), (2, Y2)):
            for zz in range(2):
                src = X.at[:, cols(2048 + zz * 1024 + lax.rem(y + k, 4) * 256, 256)]
                in_y.append(send(src, IrY.at[k - 1, zz], dev))

    def input_sum_y():
        for cp in in_y:
            cp.wait_recv()
        for zz in range(2):
            at = cols(2048 + zz * 1024 + y * 256, 256)
            total = X[:, at].astype(F32)
            for k in range(3):
                total = total + IrY[k, zz].astype(F32)
            X[:, at] = total.astype(BF16)
        in_z.append(send(X.at[:, cols(2048 + (1 - zl) * 1024 + y * 256, 256)], IrZ.at[...], Z1))

    def input_sum_z():
        in_z[0].wait_recv()
        o_in[...] = (X[:, cols(2048 + zl * 1024 + y * 256, 256)].astype(F32) + IrZ[...].astype(F32)).astype(BF16)

    g_own(0)
    g_own(1)
    g_own(2)
    for cp in x_sends:
        cp.wait_send()
    input_part(1 - c, 0)
    in_c = send(X.at[:, cols(0, 2048)], IrC.at[...], C)
    relay(5)
    relay(6)
    input_part(c, 2048)
    relay(7)
    for cp in xt_c:
        cp.wait_recv()
    input_sum_cores()
    g_forward(0)
    g_own(3)
    g_forward(1)
    g_own(4)
    down_away(0)
    down_away(1)
    p_other(0)
    g_forward(2)
    g_own(5)
    p_other(1)
    g_forward(3)
    g_own(6)
    p_other(2)
    input_sum_y()
    g_forward(4)
    p_other(3)
    g_forward(5)
    p_own(0)
    p_other(4)
    p_own(1)
    g_forward(6)
    p_other(5)
    p_own(2)
    p_other(6)
    input_sum_z()
    p_own(3)
    p_own(4)
    down_own()
    p_own(5)
    p_own(6)

    for cp in started:
        if not any(cp is other for other in x_sends):
            cp.wait_send()
    for place in ORDER:
        rel = relation(place)

        @pl.when(rel == 2)
        def _():
            reduce_copy(place, 0).wait_send()
            reduce_copy(place, 1).wait_send()

        @pl.when(lax.rem(rel, 2) == 1)
        def _():
            reduce_copy(place, 2).wait_send()
            reduce_copy(place, 3).wait_send()


def hand_out(*refs):
    src, dst, held, sems = refs[:4], refs[4:8], refs[8:12], refs[12]
    into = [pltpu.make_async_copy(src[i], held[i], sems.at[0, i]) for i in range(4)]
    out = [pltpu.make_async_copy(held[i], dst[i], sems.at[1, i]) for i in range(4)]
    for cp in into:
        cp.start()
    for i in range(4):
        into[i].wait()
        out[i].start()
    for cp in out:
        cp.wait()


def on_device(inputs, w_gate, w_up, w_down, cotangents, prefix_widths, block_rank):
    tok = inputs.shape[0]
    width, units = w_gate.shape
    anywhere = pl.BlockSpec(memory_space=pl.ANY)
    smem = pl.BlockSpec(memory_space=pltpu.SMEM)
    vmem = pl.BlockSpec(memory_space=pltpu.VMEM)
    share = width // 8
    V = pltpu.VMEM
    dma = pltpu.SemaphoreType.DMA
    scratch = [V((2, LEVELS, tok, 256), BF16) for _ in ORDER] + [
        V((tok, width), BF16),
        V((4, width // 2, 256), BF16),
        V((2, units, 512), BF16),
        V((2, 256, 2 * units), BF16),
        V((3, 512, tok), BF16),
        V((2, 512, 4 * tok), BF16),
        V((4 * tok, 2 * units), BF16),
        V((2, 4, units, 512), BF16),
        V((2, 2, units // 2, 512), BF16),
        V((2, 2, units, 512), BF16),
        V((units, 512), BF16),
        V((7, 512, 256), BF16),
        V((7, 512, 256), BF16),
        V((tok, width // 2), BF16),
        V((tok, 256), BF16),
        V((3, 2, tok, 256), BF16),
        V((tok, units), F32),
        V((tok, units), F32),
        V((tok, units), F32),
        V((units, tok), BF16),
        dma((COPIES,)),
        dma((COPIES,)),
        dma((24,)),
        dma((2, 2)),
        dma((2, 2)),
        dma((2, 2, 2)),
        dma((2, 2, 2)),
    ]
    results = pl.pallas_call(
        functools.partial(body, tok, width, units),
        out_shape=(
            jax.ShapeDtypeStruct((tok, 256), BF16),
            jax.ShapeDtypeStruct((share, units), BF16),
            jax.ShapeDtypeStruct((share, units), BF16),
            jax.ShapeDtypeStruct((units, share), BF16),
        ),
        in_specs=[smem, smem] + [anywhere] * 5,
        out_specs=(vmem,) * 4,
        scratch_shapes=scratch,
        compiler_params=pltpu.CompilerParams(
            collective_id=0, has_side_effects=True, vmem_limit_bytes=64 * 2**20),
        name="swiglu_backward",
    )(prefix_widths, block_rank, inputs, w_gate, w_up, w_down, cotangents)
    return pl.pallas_call(
        hand_out,
        out_shape=tuple(jax.ShapeDtypeStruct(r.shape, r.dtype) for r in results),
        in_specs=[anywhere] * 4,
        out_specs=(anywhere,) * 4,
        scratch_shapes=[V(r.shape, r.dtype) for r in results] + [dma((2, 4))],
        name="hand_out",
    )(*results)


def solution(mesh):
    placed = (
        P("seq", "tensor"),
        P(None, "tensor"),
        P(None, "tensor"),
        P("tensor", None),
        P(None, "seq", "tensor"),
        P(),
        P("tensor"),
    )
    return jax.shard_map(
        on_device,
        mesh=mesh,
        in_specs=placed,
        out_specs=(P("seq", "tensor"), P("seq", "tensor"), P("seq", "tensor"), P("tensor", "seq")),
        check_vma=False,
    )
```

```python
import functools

import jax
import jax.numpy as jnp
from jax import lax
from jax.experimental import pallas as pl
from jax.experimental.pallas import tpu as pltpu
from jax.sharding import PartitionSpec as P

BLOCK = 128
LEVELS = 4
MESH = pl.DeviceIdType.MESH
COPIES = 128
Z_BLOCKS = 4
F32 = jnp.float32
BF16 = jnp.bfloat16
NT = (((1,), (1,)), ((), ()))
ORDER = ((0, 0), (1, 0), (0, 3), (0, 1), (0, 2), (1, 3), (1, 1), (1, 2))


def dot(a, b):
    return jnp.dot(a, b, preferred_element_type=F32)


def dot_nt(a, b):
    return lax.dot_general(a, b, NT, preferred_element_type=F32)


def cols(start, size):
    return pl.ds(pl.multiple_of(start, 128), size)


def rows(start, size):
    return pl.ds(pl.multiple_of(start, 16), size)


def body(tok, width, units, z_rows, *refs):
    widths, rank, xin, wg, wu, wd, cot, to_in, to_g, to_u, to_d = refs[:11]
    (X, wt, wdb, wrow, XTs, XT, G, D, R1, R2, R3, Ps, Pr, IrC, IrZ, IrY, A, B, HG, hT,
     ss, rs, ls, s1, r1, s2, r2, RZ, R1A, R2A, s1a, r1a, s2a, r2a, sz, rz,
     o_in, o_g, o_u, o_d, so) = refs[11 + 8:]
    LS = {place: refs[11 + i] for i, place in enumerate(ORDER)}
    nb = units // BLOCK
    half_t, quarter = tok // 2, tok // 4
    nchunk = 2 * units // 256

    s, t = lax.axis_index("seq"), lax.axis_index("tensor")
    x, zh = lax.rem(s, 4), s // 4
    zl, y, c = t // 8, lax.rem(t // 2, 4), lax.rem(t, 2)
    at_x = lambda k: (zh * 4 + lax.rem(x + k, 4), t)
    at_y = lambda k: (s, zl * 8 + lax.rem(y + k, 4) * 2 + c)
    C = (s, t + 1 - 2 * c)
    Z1 = (s, t + 8 - 16 * zl)
    Z2 = ((1 - zh) * 4 + x, t)
    Xp, Xm, X2, Yp, Ym, Y2 = at_x(1), at_x(3), at_x(2), at_y(1), at_y(3), at_y(2)

    started = []
    local = []

    def send(src, dst, dev):
        i = len(started)
        cp = pltpu.make_async_remote_copy(
            src_ref=src, dst_ref=dst, send_sem=ss.at[i], recv_sem=rs.at[i],
            device_id=dev, device_id_type=MESH)
        cp.start()
        started.append(cp)
        return cp

    def load(src, dst):
        i = len(local)
        cp = pltpu.make_async_copy(src, dst, ls.at[i])
        cp.start()
        local.append(cp)
        return cp

    cot_loads = [load(cot.at[g], A.at[:, cols(256 * g, 256)]) for g in range(3)]
    cot_loads.append(load(cot.at[3], B.at[:, cols(0, 256)]))
    own_x = load(xin, X.at[:, cols(t * 256, 256)])

    half_w = width // 2

    def tile_half(n):
        h = n // nb
        return zl + h - 2 * zl * h

    stored = []

    def store(held, out):
        cp = pltpu.make_async_copy(held, out, so.at[len(stored)])
        cp.start()
        stored.append(cp)

    def tile_loads(n, slot):
        at, lane = rows(tile_half(n) * half_w, half_w), cols(lax.rem(n, nb) * BLOCK, BLOCK)
        return (
            pltpu.make_async_copy(wg.at[at, lane], wt.at[slot, :, cols(0, BLOCK)], ls.at[8 + 2 * slot]),
            pltpu.make_async_copy(wu.at[at, lane], wt.at[slot, :, cols(BLOCK, BLOCK)], ls.at[9 + 2 * slot]),
        )

    for slot in range(4):
        for cp in tile_loads(slot, slot):
            cp.start()

    def feature_slice(place):
        return (zl + place[0] - 2 * zl * place[0]) * 4 + lax.rem(y + place[1], 4)

    def down_load(k):
        return pltpu.make_async_copy(wd.at[:, cols(feature_slice(ORDER[k]) * 512, 512)],
                                     wdb.at[k % 2], ls.at[20 + k % 2])

    down_load(0).start()
    down_load(1).start()

    barrier = pltpu.get_barrier_semaphore()
    peers = (C, Z1, Z2, Xp, Xm, X2, Yp, Ym, Y2)
    for dev in peers:
        pl.semaphore_signal(barrier, inc=1, device_id=dev, device_id_type=MESH)
    pl.semaphore_wait(barrier, len(peers))

    def x_view(place, first, count):
        tt = feature_slice(place) * 2 + c
        return X.at[pl.ds(first * quarter, count * quarter), cols(tt * 256, 256)]

    def x_pair(place, moved, first, count):
        return x_view(place, first, count), x_view(place, first, count)

    def ls_pair(place, moved, first, count):
        levels = pl.ds(first, count)
        return LS[place].at[c, levels], LS[moved].at[c, levels]

    class Gather:
        def __init__(self, pair, cut):
            self.pair = pair
            self.cut = cut
            self.moves = {}

        def send(self, step, place, first=0, count=4, src=None):
            dz, dy = place
            moved, dev = {"C": (place, C), "Z": ((1 - dz, dy), Z1), "P": ((dz, (dy + 3) % 4), Yp),
                          "M": ((dz, (dy + 1) % 4), Ym)}[step]
            mine, there = self.pair(place, moved, first, count)
            self.moves[step, place] = send(mine if src is None else src, there, dev)

        def got(self, step, place):
            self.moves[step, place].wait_recv()

        def late_z(self, place):
            if self.cut < 4:
                self.send("Z", place, self.cut, 4 - self.cut)

        def got_late_z(self, place):
            if self.cut < 4:
                self.got("Z", place)

        def along_z(self):
            self.got("Z", (0, 0))
            self.send("P", (1, 0), 0, self.cut)
            self.send("M", (1, 0), 0, self.cut)
            self.send("C", (1, 0))

        def neighbours0(self):
            self.got("P", (0, 0))
            self.send("P", (0, 3), 0, 2)
            self.late_z((0, 3))
            self.send("C", (0, 3))
            self.got("M", (0, 0))
            self.send("M", (0, 1), 2, 2)
            self.late_z((0, 1))
            self.send("C", (0, 1))

        def opposite0(self):
            self.got("P", (0, 3))
            self.got("M", (0, 1))
            self.late_z((0, 2))
            self.send("C", (0, 2))

        def neighbours1(self):
            self.got("P", (1, 0))
            self.send("P", (1, 3), 0, self.cut // 2)
            self.got("M", (1, 0))
            self.send("M", (1, 1), self.cut // 2, self.cut // 2)
            self.got_late_z((0, 3))
            self.send("C", (1, 3))
            self.got_late_z((0, 1))
            self.send("C", (1, 1))

        def opposite1(self):
            self.got("P", (1, 3))
            self.got("M", (1, 1))
            self.got_late_z((0, 2))
            self.send("C", (1, 2))

    gx, gl = Gather(x_pair, 4), Gather(ls_pair, 2)
    for step in "ZPMC":
        gx.send(step, (0, 0), src=xin)

    for cp in cot_loads:
        cp.wait()
    total = A[:, 0:256]
    own = LS[(0, 0)]
    own[c, 0] = total.astype(BF16)
    for g in range(1, LEVELS):
        total = total + (A[:, 256 * g:256 * g + 256] if g < 3 else B[:, 0:256])
        own[c, g] = total.astype(BF16)

    gx.along_z()
    gl.send("Z", (0, 0))
    gl.send("C", (0, 0))
    gx.neighbours0()
    gx.opposite0()
    gx.neighbours1()
    gl.send("P", (0, 0))
    gl.send("M", (0, 0))
    own_x.wait()
    for dy in range(4):
        gx.got("C", (0, dy))

    def forward_part(n):
        slot = lax.rem(n, 4)
        for cp in tile_loads(n, slot):
            cp.wait()
        return dot(X[:, cols(tile_half(n) * half_w, half_w)], wt[slot])

    def tile_next(n):
        @pl.when(n + 4 < 2 * nb)
        def _():
            for cp in tile_loads(n + 4, lax.rem(n, 4)):
                cp.start()

    def forward_first(b, _):
        both = forward_part(b)
        tile_next(b)
        at = cols(b * BLOCK, BLOCK)
        A[:, at] = both[:, :BLOCK]
        B[:, at] = both[:, BLOCK:]
        return 0

    def forward(b, _):
        both = forward_part(b + nb)
        tile_next(b + nb)
        at = cols(b * BLOCK, BLOCK)
        gate, up = both[:, :BLOCK] + A[:, at], both[:, BLOCK:] + B[:, at]
        sigma = jax.nn.sigmoid(gate)
        active = gate * sigma
        A[:, at] = up * sigma * (1.0 + gate * (1.0 - sigma))
        B[:, at] = active
        hT[rows(b * BLOCK, BLOCK), :] = jnp.transpose((active * up).astype(BF16))
        return 0

    lax.fori_loop(0, nb, forward_first, 0)
    gx.opposite1()
    for dy in range(4):
        gx.got("C", (1, dy))
    x_sends = list(gx.moves.values())

    def transposed(zz):
        return jnp.transpose(X[:, cols((zz * 4 + x) * 512, 512)])

    share = 512 // 8
    mine = rows((zl * 4 + y) * share, share)
    far_tokens = pl.ds(tok, 3 * tok)
    x_moves = []
    for k, dev in ((1, Xp), (3, Xm), (2, X2)):
        lanes = cols((c * 4 + lax.rem(x + k, 4)) * 512 + (zl * 2 + y // 2) * 128, 128)
        block = jnp.transpose(X[:, lanes])
        XTs[k - 1] = jnp.where(lax.rem(y, 2) == 0, block[:share], block[share:])
        x_moves.append(send(XTs.at[k - 1], XT.at[c, mine, cols((4 - k) * tok, tok)], dev))
    for zz in range(2):
        XT[zz, :, 0:tok] = transposed(zz)
    xt_moves = {}

    def xt_along_z():
        for cp in x_moves:
            cp.wait_recv()
        piece = XT.at[c, mine, far_tokens]
        xt_moves["Z"] = send(piece, piece, Z1)

    def xt_around_y():
        xt_moves["Z"].wait_recv()
        for k, dev in ((1, Yp), (3, Ym), (2, Y2)):
            for h in range(2):
                piece = XT.at[c, rows((h * 4 + y) * share, share), far_tokens]
                xt_moves[k, h] = send(piece, piece, dev)

    def xt_cores():
        for k in (1, 3, 2):
            for h in range(2):
                xt_moves[k, h].wait_recv()
        piece = XT.at[c, :, far_tokens]
        xt_moves["C"] = send(piece, piece, C)

    lax.fori_loop(0, nb, forward, 0)

    def relation(place):
        return lax.rem(y + place[1] - x + 4, 4)

    def owner_z(place):
        return zl + place[0] - 2 * zl * place[0]

    early = (0, z_rows // 2, R1A, R2A, s1a, r1a, s2a, r2a)
    late = (z_rows, (units - z_rows) // 2, R1, R2, s1, r1, s2, r2)

    def at_owner(ref, part, zz, *index):
        return ref.at[index] if part is early else ref.at[(zz, *index)]

    def reduce_copy(part, place, kind):
        base, half, one, two, send1, recv1, send2, recv2 = part
        dz, dy = place
        zz = owner_z(place)
        if kind < 2:
            return pltpu.make_async_remote_copy(
                src_ref=D.at[dz, dy, pl.ds(base + kind * half, half)],
                dst_ref=at_owner(one, part, zz, kind),
                send_sem=at_owner(send1, part, zz, kind), recv_sem=at_owner(recv1, part, zz, kind),
                device_id=Xp if kind == 0 else Xm, device_id_type=MESH)
        rel = relation(place)
        side = rel // 2
        h = 1 - side if kind == 2 else side
        return pltpu.make_async_remote_copy(
            src_ref=D.at[dz, dy, rows(base + h * half, half)],
            dst_ref=at_owner(two, part, zz, side, rows(h * half, half)),
            send_sem=at_owner(send2, part, zz, side, kind - 2),
            recv_sem=at_owner(recv2, part, zz, side, kind - 2),
            device_id=at_x(rel), device_id_type=MESH)

    def reduce_first(part, place):
        rel = relation(place)

        @pl.when(rel == 2)
        def _():
            reduce_copy(part, place, 0).start()
            reduce_copy(part, place, 1).start()

        @pl.when(lax.rem(rel, 2) == 1)
        def _():
            reduce_copy(part, place, 2).start()

    def reduce_relay(part, place):
        base, half, one, two, send1, recv1, send2, recv2 = part
        dz, dy = place
        rel = relation(place)
        zz = owner_z(place)
        side = rel // 2

        @pl.when(lax.rem(rel, 2) == 1)
        def _():
            pltpu.make_async_remote_copy(
                src_ref=D.at[dz, dy, pl.ds(base, half)], dst_ref=at_owner(one, part, zz, side),
                send_sem=at_owner(send1, part, zz, side), recv_sem=at_owner(recv1, part, zz, side),
                device_id=Xp, device_id_type=MESH).wait_recv()
            span = rows(base + side * half, half)
            D[dz, dy, span, :] = (D[dz, dy, span, :].astype(F32)
                                  + at_owner(one, part, zz, side)[...].astype(F32)).astype(BF16)
            reduce_copy(part, place, 3).start()

    def reduce_drain(part, place):
        rel = relation(place)

        @pl.when(rel == 2)
        def _():
            reduce_copy(part, place, 0).wait_send()
            reduce_copy(part, place, 1).wait_send()

        @pl.when(lax.rem(rel, 2) == 1)
        def _():
            reduce_copy(part, place, 2).wait_send()
            reduce_copy(part, place, 3).wait_send()

    def z_copy(place):
        dz, dy = place
        return pltpu.make_async_remote_copy(
            src_ref=D.at[dz, dy, pl.ds(0, z_rows)], dst_ref=RZ.at[dy],
            send_sem=sz.at[dy], recv_sem=rz.at[dy], device_id=Z2, device_id_type=MESH)

    def early_send(k):
        if not z_rows:
            return

        @pl.when(owner_z(ORDER[k]) != zh)
        def _():
            z_copy(ORDER[k]).start()

    def early_first(k):
        if not z_rows:
            return
        place = ORDER[k]
        dz, dy = place

        @pl.when(owner_z(place) == zh)
        def _():
            z_copy(place).wait_recv()
            span = pl.ds(0, z_rows)
            D[dz, dy, span, :] = (D[dz, dy, span, :].astype(F32) + RZ[dy].astype(F32)).astype(BF16)
            reduce_first(early, place)

    def early_relay(k):
        if not z_rows:
            return
        @pl.when(owner_z(ORDER[k]) == zh)
        def _():
            reduce_relay(early, ORDER[k])

    def relay(k):
        reduce_relay(late, ORDER[k])

    def slice_work(k):
        place = ORDER[k]
        dz, dy = place
        src = LS[place]
        down_load(k).wait()

        def step(b, _):
            used = sum((rank[b] * BLOCK < widths[g]).astype(jnp.int32) for g in range(LEVELS))
            level = jnp.maximum(used - 1, 0)
            l0, l1 = src[0, level], src[1, level]
            at = rows(b * BLOCK, BLOCK)
            h = hT[at, :]
            D[dz, dy, at, 0:256] = dot(h, l0).astype(BF16)
            D[dz, dy, at, 256:512] = dot(h, l1).astype(BF16)
            part = dot_nt(l0, wdb[k % 2, at, 0:256]) + dot_nt(l1, wdb[k % 2, at, 256:512])
            lane = cols(b * BLOCK, BLOCK)
            HG[:, lane] = part if k == 0 else HG[:, lane] + part
            return 0

        lax.fori_loop(0, nb, step, 0)
        if k + 2 < len(ORDER):
            down_load(k + 2).start()
        if k < 7:
            reduce_first(late, place)

    def row_loads(n, slot):
        core = jnp.where(n < 8, 1 - c, c)
        at = rows((2 * lax.rem(n, 8) + core) * 256, 256)
        return (
            pltpu.make_async_copy(wg.at[at, :], wrow.at[slot, :, cols(0, units)], ls.at[16 + 2 * slot]),
            pltpu.make_async_copy(wu.at[at, :], wrow.at[slot, :, cols(units, units)], ls.at[17 + 2 * slot]),
        )

    def input_part(first):
        def step(n, _):
            slot = lax.rem(n, 2)
            for cp in row_loads(n, slot):
                cp.wait()
            X[:, cols(n * 256, 256)] = dot_nt(G[0:tok, :], wrow[slot]).astype(BF16)

            @pl.when(n + 2 < 16)
            def _():
                for cp in row_loads(n + 2, slot):
                    cp.start()
            return 0

        lax.fori_loop(first, first + 4, step, 0)

    gl.along_z()
    gl.got("C", (0, 0))
    slice_work(0)
    xt_along_z()
    gl.neighbours0()
    gl.got("C", (1, 0))
    slice_work(1)
    gl.got("C", (0, 3))
    slice_work(2)
    gl.got("C", (0, 1))
    slice_work(3)
    gl.opposite0()
    for k in range(4):
        early_send(k)
    relay(0)
    gl.got("C", (0, 2))
    slice_work(4)
    early_send(4)
    gl.neighbours1()
    xt_around_y()
    relay(1)
    gl.got("C", (1, 3))
    slice_work(5)
    early_send(5)
    gl.got("C", (1, 1))
    slice_work(6)
    early_send(6)
    gl.opposite1()
    relay(2)
    relay(3)
    for slot in range(2):
        for cp in row_loads(slot, slot):
            cp.start()
    gl.got("C", (1, 2))
    slice_work(7)
    early_send(7)

    def grads(b, _):
        at = cols(b * BLOCK, BLOCK)
        hg = HG[:, at]
        G[0:tok, at] = (hg * A[:, at]).astype(BF16)
        G[0:tok, cols(units + b * BLOCK, BLOCK)] = (hg * B[:, at]).astype(BF16)
        return 0

    lax.fori_loop(0, nb, grads, 0)

    from_m, from_p, far = {}, {}, {}

    def g_own(j):
        at = cols(j * 256, 256)
        src = G.at[pl.ds(0, tok), at]
        from_m[j] = send(src, G.at[pl.ds(3 * tok, tok), at], Xp)
        from_p[j] = send(src, G.at[pl.ds(tok, tok), at], Xm)

    def g_forward(j):
        at = cols(j * 256, 256)
        from_m[j].wait_recv()
        far[j, 0] = send(G.at[pl.ds(3 * tok, half_t), at], G.at[pl.ds(2 * tok, half_t), at], Xp)
        from_p[j].wait_recv()
        far[j, 1] = send(G.at[pl.ds(tok + half_t, half_t), at],
                         G.at[pl.ds(2 * tok + half_t, half_t), at], Xm)

    p_sent = {}

    def p_other(j):
        far[j, 0].wait_recv()
        far[j, 1].wait_recv()
        at = cols(j * 256, 256)
        for h in range(2):
            Ps[j, pl.ds(256 * h, 256), :] = dot(XT[1 - zh, pl.ds(256 * h, 256), :], G[:, at]).astype(BF16)
        p_sent[j] = send(Ps.at[j], Pr.at[j], Z2)

    def p_own(j):
        p_sent[j].wait_recv()
        at = cols(j * 256, 256)
        for h in range(2):
            r = pl.ds(256 * h, 256)
            out = (dot(XT[zh, r, :], G[:, at]) + Pr[j, r, :].astype(F32)).astype(BF16)
            for i in range(2):
                lane = j * 256 + i * BLOCK
                target, lane = (o_g, lane) if lane < units else (o_u, lane - units)
                target[r, lane:lane + BLOCK] = out[:, i * BLOCK:(i + 1) * BLOCK]
        for i in range(2):
            lane = j * 256 + i * BLOCK
            held, out, lane = (o_g, to_g, lane) if lane < units else (o_u, to_u, lane - units)
            store(held.at[:, cols(lane, BLOCK)], out.at[:, cols(lane, BLOCK)])

    def sum_x(part, zz):
        base, half, one, two, send1, recv1, send2, recv2 = part
        for side in range(2):
            for i in range(2):
                pltpu.make_async_remote_copy(
                    src_ref=D.at[0, 0, pl.ds(base, half)],
                    dst_ref=at_owner(two, part, zz, side, pl.ds(0, half)),
                    send_sem=at_owner(send2, part, zz, side, i), recv_sem=at_owner(recv2, part, zz, side, i),
                    device_id=Xp, device_id_type=MESH).wait_recv()

    def down_place(zz):
        return zl + zz - 2 * zl * zz, lax.rem(x - y + 4, 4)

    down_z = []

    def down_away():
        zz = 1 - zh
        sum_x(late, zz)
        dz, dy = down_place(zz)
        at = pl.ds(z_rows, units - z_rows)
        D[dz, dy, at, :] = (D[dz, dy, at, :].astype(F32) + R2[zz, 0].astype(F32)
                            + R2[zz, 1].astype(F32)).astype(BF16)
        down_z.append(send(D.at[dz, dy, at], R3.at[...], Z2))

    def down_own_early():
        if not z_rows:
            return
        sum_x(early, zh)
        dz, dy = down_place(zh)
        at = pl.ds(0, z_rows)
        o_d[at, :] = (D[dz, dy, at, :].astype(F32) + R2A[0].astype(F32) + R2A[1].astype(F32)).astype(BF16)
        store(o_d.at[at], to_d.at[at])

    def down_own():
        sum_x(late, zh)
        for cp in down_z:
            cp.wait_recv()
        dz, dy = down_place(zh)
        at = pl.ds(z_rows, units - z_rows)
        o_d[at, :] = (D[dz, dy, at, :].astype(F32) + R2[zh, 0].astype(F32) + R2[zh, 1].astype(F32)
                      + R3[...].astype(F32)).astype(BF16)
        store(o_d.at[at], to_d.at[at])

    in_y, in_z = [], []

    def input_sum_cores():
        in_c.wait_recv()
        for i in range(8):
            at = cols(2048 + 256 * i, 256)
            X[:, at] = (X[:, at].astype(F32) + IrC[:, cols(256 * i, 256)].astype(F32)).astype(BF16)
        for k, dev in ((1, Yp), (3, Ym), (2, Y2)):
            for zz in range(2):
                src = X.at[:, cols(2048 + zz * 1024 + lax.rem(y + k, 4) * 256, 256)]
                in_y.append(send(src, IrY.at[k - 1, zz], dev))

    def input_sum_y():
        for cp in in_y:
            cp.wait_recv()
        for zz in range(2):
            at = cols(2048 + zz * 1024 + y * 256, 256)
            total = X[:, at].astype(F32)
            for k in range(3):
                total = total + IrY[k, zz].astype(F32)
            X[:, at] = total.astype(BF16)
        in_z.append(send(X.at[:, cols(2048 + (1 - zl) * 1024 + y * 256, 256)], IrZ.at[...], Z1))

    def input_sum_z():
        in_z[0].wait_recv()
        o_in[...] = (X[:, cols(2048 + zl * 1024 + y * 256, 256)].astype(F32) + IrZ[...].astype(F32)).astype(BF16)
        store(o_in, to_in)

    g_own(0)
    g_own(1)
    reduce_first(late, ORDER[7])
    for cp in x_sends:
        cp.wait_send()
    input_part(0)
    relay(4)
    relay(5)
    g_forward(0)
    g_own(2)
    input_part(4)
    in_c = send(X.at[:, cols(0, 2048)], IrC.at[...], C)
    xt_cores()
    relay(6)
    g_forward(1)
    g_own(3)
    early_first(0)
    early_first(1)
    xt_moves["C"].wait_recv()
    p_other(0)
    input_part(8)
    g_forward(2)
    g_own(4)
    p_other(1)
    input_part(12)
    input_sum_cores()
    relay(7)
    early_first(2)
    early_first(3)
    early_relay(0)
    early_relay(1)
    g_forward(3)
    g_own(5)
    p_other(2)
    early_first(4)
    early_first(5)
    early_first(6)
    early_first(7)
    early_relay(2)
    early_relay(3)
    g_forward(4)
    g_own(6)
    p_other(3)
    p_own(0)
    early_relay(4)
    early_relay(5)
    early_relay(6)
    early_relay(7)
    g_forward(5)
    down_away()
    p_other(4)
    p_own(1)
    input_sum_y()
    g_forward(6)
    p_other(5)
    p_own(2)
    p_other(6)
    input_sum_z()
    p_own(3)
    p_own(4)
    down_own_early()
    p_own(5)
    down_own()
    p_own(6)

    for cp in stored:
        cp.wait()
    for cp in started:
        if not any(cp is other for other in x_sends):
            cp.wait_send()
    for place in ORDER:
        reduce_drain(late, place)
        if not z_rows:
            continue

        @pl.when(owner_z(place) == zh)
        def _():
            reduce_drain(early, place)

        @pl.when(owner_z(place) != zh)
        def _():
            z_copy(place).wait_send()


def hand_out(*refs):
    src, dst, held, sems = refs[:4], refs[4:8], refs[8:12], refs[12]
    into = [pltpu.make_async_copy(src[i], held[i], sems.at[0, i]) for i in range(4)]
    out = [pltpu.make_async_copy(held[i], dst[i], sems.at[1, i]) for i in range(4)]
    for cp in into:
        cp.start()
    for i in range(4):
        into[i].wait()
        out[i].start()
    for cp in out:
        cp.wait()


def on_device(inputs, w_gate, w_up, w_down, cotangents, prefix_widths, block_rank):
    tok = inputs.shape[0]
    width, units = w_gate.shape
    anywhere = pl.BlockSpec(memory_space=pl.ANY)
    smem = pl.BlockSpec(memory_space=pltpu.SMEM)
    share = width // 8
    z_rows = Z_BLOCKS * BLOCK
    held = max(z_rows, 32)
    V = pltpu.VMEM
    dma = pltpu.SemaphoreType.DMA
    scratch = [V((2, LEVELS, tok, 256), BF16) for _ in ORDER] + [
        V((tok, width), BF16),
        V((4, width // 2, 256), BF16),
        V((2, units, 512), BF16),
        V((2, 256, 2 * units), BF16),
        V((3, 64, tok), BF16),
        V((2, 512, 4 * tok), BF16),
        V((4 * tok, 2 * units), BF16),
        V((2, 4, units, 512), BF16),
        V((2, 2, (units - z_rows) // 2, 512), BF16),
        V((2, 2, units - z_rows, 512), BF16),
        V((units - z_rows, 512), BF16),
        V((7, 512, 256), BF16),
        V((7, 512, 256), BF16),
        V((tok, width // 2), BF16),
        V((tok, 256), BF16),
        V((3, 2, tok, 256), BF16),
        V((tok, units), F32),
        V((tok, units), F32),
        V((tok, units), F32),
        V((units, tok), BF16),
        dma((COPIES,)),
        dma((COPIES,)),
        dma((24,)),
        dma((2, 2)),
        dma((2, 2)),
        dma((2, 2, 2)),
        dma((2, 2, 2)),
        V((4, held, 512), BF16),
        V((2, held // 2, 512), BF16),
        V((2, held, 512), BF16),
        dma((2,)),
        dma((2,)),
        dma((2, 2)),
        dma((2, 2)),
        dma((4,)),
        dma((4,)),
        V((tok, 256), BF16),
        V((share, units), BF16),
        V((share, units), BF16),
        V((units, share), BF16),
        dma((24,)),
    ]
    results = pl.pallas_call(
        functools.partial(body, tok, width, units, z_rows),
        out_shape=(
            jax.ShapeDtypeStruct((tok, 256), BF16),
            jax.ShapeDtypeStruct((share, units), BF16),
            jax.ShapeDtypeStruct((share, units), BF16),
            jax.ShapeDtypeStruct((units, share), BF16),
        ),
        in_specs=[smem, smem] + [anywhere] * 5,
        out_specs=(anywhere,) * 4,
        scratch_shapes=scratch,
        compiler_params=pltpu.CompilerParams(
            collective_id=0, has_side_effects=True, vmem_limit_bytes=64 * 2**20),
        name="swiglu_backward",
    )(prefix_widths, block_rank, inputs, w_gate, w_up, w_down, cotangents)
    return pl.pallas_call(
        hand_out,
        out_shape=tuple(jax.ShapeDtypeStruct(r.shape, r.dtype) for r in results),
        in_specs=[anywhere] * 4,
        out_specs=(anywhere,) * 4,
        scratch_shapes=[V(r.shape, r.dtype) for r in results] + [dma((2, 4))],
        name="hand_out",
    )(*results)


def solution(mesh):
    placed = (
        P("seq", "tensor"),
        P(None, "tensor"),
        P(None, "tensor"),
        P("tensor", None),
        P(None, "seq", "tensor"),
        P(),
        P("tensor"),
    )
    return jax.shard_map(
        on_device,
        mesh=mesh,
        in_specs=placed,
        out_specs=(P("seq", "tensor"), P("seq", "tensor"), P("seq", "tensor"), P("tensor", "seq")),
        check_vma=False,
    )
```

```python
import functools

import jax
import jax.numpy as jnp
from jax import lax
from jax.experimental import pallas as pl
from jax.experimental.pallas import tpu as pltpu
from jax.sharding import PartitionSpec as P

BLOCK = 128
LEVELS = 4
MESH = pl.DeviceIdType.MESH
COPIES = 128
Z_BLOCKS = 4
F32 = jnp.float32
BF16 = jnp.bfloat16
NT = (((1,), (1,)), ((), ()))
ORDER = ((0, 0), (1, 0), (0, 3), (0, 1), (0, 2), (1, 3), (1, 1), (1, 2))


def dot(a, b):
    return jnp.dot(a, b, preferred_element_type=F32)


def dot_nt(a, b):
    return lax.dot_general(a, b, NT, preferred_element_type=F32)


def cols(start, size):
    return pl.ds(pl.multiple_of(start, 128), size)


def rows(start, size):
    return pl.ds(pl.multiple_of(start, 16), size)


def body(tok, width, units, z_rows, *refs):
    widths, rank, xin, wg, wu, wd, cot, to_in, to_g, to_u, to_d = refs[:11]
    (X, wt, wdb, wrow, XTs, XT, G, D, R1, R2, R3, Ps, Pr, IrC, IrZ, IrY, A, B, HG, hT,
     ss, rs, ls, s1, r1, s2, r2, RZ, R1A, R2A, s1a, r1a, s2a, r2a, sz, rz,
     o_in, o_g, o_u, o_d, so) = refs[11 + 8:]
    LS = {place: refs[11 + i] for i, place in enumerate(ORDER)}
    nb = units // BLOCK
    half_t, quarter = tok // 2, tok // 4
    nchunk = 2 * units // 256

    s, t = lax.axis_index("seq"), lax.axis_index("tensor")
    x, zh = lax.rem(s, 4), s // 4
    zl, y, c = t // 8, lax.rem(t // 2, 4), lax.rem(t, 2)
    at_x = lambda k: (zh * 4 + lax.rem(x + k, 4), t)
    at_y = lambda k: (s, zl * 8 + lax.rem(y + k, 4) * 2 + c)
    C = (s, t + 1 - 2 * c)
    Z1 = (s, t + 8 - 16 * zl)
    Z2 = ((1 - zh) * 4 + x, t)
    Xp, Xm, X2, Yp, Ym, Y2 = at_x(1), at_x(3), at_x(2), at_y(1), at_y(3), at_y(2)

    started = []
    local = []

    def send(src, dst, dev):
        i = len(started)
        cp = pltpu.make_async_remote_copy(
            src_ref=src, dst_ref=dst, send_sem=ss.at[i], recv_sem=rs.at[i],
            device_id=dev, device_id_type=MESH)
        cp.start()
        started.append(cp)
        return cp

    def load(src, dst):
        i = len(local)
        cp = pltpu.make_async_copy(src, dst, ls.at[i])
        cp.start()
        local.append(cp)
        return cp

    cot_loads = [load(cot.at[g], A.at[:, cols(256 * g, 256)]) for g in range(3)]
    cot_loads.append(load(cot.at[3], B.at[:, cols(0, 256)]))
    own_x = load(xin, X.at[:, cols(t * 256, 256)])

    half_w = width // 2

    def tile_half(n):
        h = n // nb
        return zl + h - 2 * zl * h

    stored = []

    def store(held, out):
        cp = pltpu.make_async_copy(held, out, so.at[len(stored)])
        cp.start()
        stored.append(cp)

    def tile_loads(n, slot):
        at, lane = rows(tile_half(n) * half_w, half_w), cols(lax.rem(n, nb) * BLOCK, BLOCK)
        return (
            pltpu.make_async_copy(wg.at[at, lane], wt.at[slot, :, cols(0, BLOCK)], ls.at[8 + 2 * slot]),
            pltpu.make_async_copy(wu.at[at, lane], wt.at[slot, :, cols(BLOCK, BLOCK)], ls.at[9 + 2 * slot]),
        )

    for slot in range(4):
        for cp in tile_loads(slot, slot):
            cp.start()

    def feature_slice(place):
        return (zl + place[0] - 2 * zl * place[0]) * 4 + lax.rem(y + place[1], 4)

    def down_load(k):
        return pltpu.make_async_copy(wd.at[:, cols(feature_slice(ORDER[k]) * 512, 512)],
                                     wdb.at[k % 2], ls.at[20 + k % 2])

    down_load(0).start()
    down_load(1).start()

    barrier = pltpu.get_barrier_semaphore()
    peers = (C, Z1, Z2, Xp, Xm, X2, Yp, Ym, Y2)
    for dev in peers:
        pl.semaphore_signal(barrier, inc=1, device_id=dev, device_id_type=MESH)
    pl.semaphore_wait(barrier, len(peers))

    def x_view(place, first, count):
        tt = feature_slice(place) * 2 + c
        return X.at[pl.ds(first * quarter, count * quarter), cols(tt * 256, 256)]

    def x_pair(place, moved, first, count):
        return x_view(place, first, count), x_view(place, first, count)

    def ls_pair(place, moved, first, count):
        levels = pl.ds(first, count)
        return LS[place].at[c, levels], LS[moved].at[c, levels]

    class Gather:
        def __init__(self, pair, cut):
            self.pair = pair
            self.cut = cut
            self.moves = {}

        def send(self, step, place, first=0, count=4, src=None):
            dz, dy = place
            moved, dev = {"C": (place, C), "Z": ((1 - dz, dy), Z1), "P": ((dz, (dy + 3) % 4), Yp),
                          "M": ((dz, (dy + 1) % 4), Ym)}[step[0]]
            mine, there = self.pair(place, moved, first, count)
            self.moves[step, place] = send(mine if src is None else src, there, dev)

        def got(self, step, place):
            self.moves[step, place].wait_recv()

        def late_z(self, place):
            if self.cut < 4:
                self.send("Z", place, self.cut, 4 - self.cut)

        def got_late_z(self, place):
            if self.cut < 4:
                self.got("Z", place)

        def along_z(self):
            self.got("Z", (0, 0))
            self.send("P", (1, 0), 0, self.cut)
            self.send("M", (1, 0), 0, self.cut)
            self.send("C", (1, 0))

        def neighbours0_late(self):
            self.got("P2", (0, 0))
            self.late_z((0, 3))
            self.got("M2", (0, 0))
            self.send("M", (0, 1), 2, 2)
            self.late_z((0, 1))

        def neighbours0(self):
            self.got("P", (0, 0))
            self.send("P", (0, 3), 0, 2)
            self.send("C", (0, 3))
            self.got("M", (0, 0))
            if self.cut == 4:
                self.send("M", (0, 1), 2, 2)
            self.send("C", (0, 1))

        def opposite0_late(self):
            self.got("M", (0, 1))
            self.late_z((0, 2))

        def opposite0(self):
            self.got("P", (0, 3))
            if self.cut == 4:
                self.got("M", (0, 1))
            self.send("C", (0, 2))

        def neighbours1(self):
            self.got("P", (1, 0))
            self.send("P", (1, 3), 0, self.cut // 2)
            self.got("M", (1, 0))
            self.send("M", (1, 1), self.cut // 2, self.cut // 2)
            self.got_late_z((0, 3))
            self.send("C", (1, 3))
            self.got_late_z((0, 1))
            self.send("C", (1, 1))

        def opposite1(self):
            self.got("P", (1, 3))
            self.got("M", (1, 1))
            self.got_late_z((0, 2))
            self.send("C", (1, 2))

    gx, gl = Gather(x_pair, 4), Gather(ls_pair, 2)
    for step in "ZPMC":
        gx.send(step, (0, 0), src=xin)

    for cp in cot_loads:
        cp.wait()
    total = A[:, 0:256]
    own = LS[(0, 0)]
    own[c, 0] = total.astype(BF16)
    for g in range(1, LEVELS):
        total = total + (A[:, 256 * g:256 * g + 256] if g < 3 else B[:, 0:256])
        own[c, g] = total.astype(BF16)

    gx.along_z()
    gl.send("Z", (0, 0))
    gl.send("C", (0, 0))
    gx.neighbours0()
    gx.opposite0()
    gx.neighbours1()
    gl.send("P2", (0, 0), 2, 2)
    gl.send("M2", (0, 0), 2, 2)
    gl.send("P", (0, 0), 0, 2)
    gl.send("M", (0, 0), 0, 2)
    own_x.wait()
    for dy in range(4):
        gx.got("C", (0, dy))

    def forward_part(n):
        slot = lax.rem(n, 4)
        for cp in tile_loads(n, slot):
            cp.wait()
        return dot(X[:, cols(tile_half(n) * half_w, half_w)], wt[slot])

    def tile_next(n):
        @pl.when(n + 4 < 2 * nb)
        def _():
            for cp in tile_loads(n + 4, lax.rem(n, 4)):
                cp.start()

    def forward_first(b, _):
        both = forward_part(b)
        tile_next(b)
        at = cols(b * BLOCK, BLOCK)
        A[:, at] = both[:, :BLOCK]
        B[:, at] = both[:, BLOCK:]
        return 0

    def forward(b, _):
        both = forward_part(b + nb)
        tile_next(b + nb)
        at = cols(b * BLOCK, BLOCK)
        gate, up = both[:, :BLOCK] + A[:, at], both[:, BLOCK:] + B[:, at]
        sigma = jax.nn.sigmoid(gate)
        active = gate * sigma
        A[:, at] = up * sigma * (1.0 + gate * (1.0 - sigma))
        B[:, at] = active
        hT[rows(b * BLOCK, BLOCK), :] = jnp.transpose((active * up).astype(BF16))
        return 0

    lax.fori_loop(0, nb, forward_first, 0)
    gx.opposite1()
    for dy in range(4):
        gx.got("C", (1, dy))
    x_sends = list(gx.moves.values())

    def transposed(zz):
        return jnp.transpose(X[:, cols((zz * 4 + x) * 512, 512)])

    share = 512 // 8
    mine = rows((zl * 4 + y) * share, share)
    far_tokens = pl.ds(tok, 3 * tok)
    x_moves = []
    for k, dev in ((1, Xp), (3, Xm), (2, X2)):
        lanes = cols((c * 4 + lax.rem(x + k, 4)) * 512 + (zl * 2 + y // 2) * 128, 128)
        block = jnp.transpose(X[:, lanes])
        XTs[k - 1] = jnp.where(lax.rem(y, 2) == 0, block[:share], block[share:])
        x_moves.append(send(XTs.at[k - 1], XT.at[c, mine, cols((4 - k) * tok, tok)], dev))
    for zz in range(2):
        XT[zz, :, 0:tok] = transposed(zz)
    xt_moves = {}

    def xt_along_z():
        for cp in x_moves:
            cp.wait_recv()
        piece = XT.at[c, mine, far_tokens]
        xt_moves["Z"] = send(piece, piece, Z1)

    def xt_around_y():
        xt_moves["Z"].wait_recv()
        for k, dev in ((1, Yp), (3, Ym), (2, Y2)):
            for h in range(2):
                piece = XT.at[c, rows((h * 4 + y) * share, share), far_tokens]
                xt_moves[k, h] = send(piece, piece, dev)

    def xt_cores():
        for k in (1, 3, 2):
            for h in range(2):
                xt_moves[k, h].wait_recv()
        piece = XT.at[c, :, far_tokens]
        xt_moves["C"] = send(piece, piece, C)

    lax.fori_loop(0, nb, forward, 0)

    def relation(place):
        return lax.rem(y + place[1] - x + 4, 4)

    def owner_z(place):
        return zl + place[0] - 2 * zl * place[0]

    early = (0, z_rows // 2, R1A, R2A, s1a, r1a, s2a, r2a)
    late = (z_rows, (units - z_rows) // 2, R1, R2, s1, r1, s2, r2)

    def at_owner(ref, part, zz, *index):
        return ref.at[index] if part is early else ref.at[(zz, *index)]

    def reduce_copy(part, place, kind):
        base, half, one, two, send1, recv1, send2, recv2 = part
        dz, dy = place
        zz = owner_z(place)
        if kind < 2:
            return pltpu.make_async_remote_copy(
                src_ref=D.at[dz, dy, pl.ds(base + kind * half, half)],
                dst_ref=at_owner(one, part, zz, kind),
                send_sem=at_owner(send1, part, zz, kind), recv_sem=at_owner(recv1, part, zz, kind),
                device_id=Xp if kind == 0 else Xm, device_id_type=MESH)
        rel = relation(place)
        side = rel // 2
        h = 1 - side if kind == 2 else side
        return pltpu.make_async_remote_copy(
            src_ref=D.at[dz, dy, rows(base + h * half, half)],
            dst_ref=at_owner(two, part, zz, side, rows(h * half, half)),
            send_sem=at_owner(send2, part, zz, side, kind - 2),
            recv_sem=at_owner(recv2, part, zz, side, kind - 2),
            device_id=at_x(rel), device_id_type=MESH)

    def reduce_first(part, place):
        rel = relation(place)

        @pl.when(rel == 2)
        def _():
            reduce_copy(part, place, 0).start()
            reduce_copy(part, place, 1).start()

        @pl.when(lax.rem(rel, 2) == 1)
        def _():
            reduce_copy(part, place, 2).start()

    def reduce_relay(part, place):
        base, half, one, two, send1, recv1, send2, recv2 = part
        dz, dy = place
        rel = relation(place)
        zz = owner_z(place)
        side = rel // 2

        @pl.when(lax.rem(rel, 2) == 1)
        def _():
            pltpu.make_async_remote_copy(
                src_ref=D.at[dz, dy, pl.ds(base, half)], dst_ref=at_owner(one, part, zz, side),
                send_sem=at_owner(send1, part, zz, side), recv_sem=at_owner(recv1, part, zz, side),
                device_id=Xp, device_id_type=MESH).wait_recv()
            span = rows(base + side * half, half)
            D[dz, dy, span, :] = (D[dz, dy, span, :].astype(F32)
                                  + at_owner(one, part, zz, side)[...].astype(F32)).astype(BF16)
            reduce_copy(part, place, 3).start()

    def reduce_drain(part, place):
        rel = relation(place)

        @pl.when(rel == 2)
        def _():
            reduce_copy(part, place, 0).wait_send()
            reduce_copy(part, place, 1).wait_send()

        @pl.when(lax.rem(rel, 2) == 1)
        def _():
            reduce_copy(part, place, 2).wait_send()
            reduce_copy(part, place, 3).wait_send()

    def z_copy(place):
        dz, dy = place
        return pltpu.make_async_remote_copy(
            src_ref=D.at[dz, dy, pl.ds(0, z_rows)], dst_ref=RZ.at[dy],
            send_sem=sz.at[dy], recv_sem=rz.at[dy], device_id=Z2, device_id_type=MESH)

    def early_send(k):
        if not z_rows:
            return

        @pl.when(owner_z(ORDER[k]) != zh)
        def _():
            z_copy(ORDER[k]).start()

    def early_first(k):
        if not z_rows:
            return
        place = ORDER[k]
        dz, dy = place

        @pl.when(owner_z(place) == zh)
        def _():
            z_copy(place).wait_recv()
            span = pl.ds(0, z_rows)
            D[dz, dy, span, :] = (D[dz, dy, span, :].astype(F32) + RZ[dy].astype(F32)).astype(BF16)
            reduce_first(early, place)

    def early_relay(k):
        if not z_rows:
            return
        @pl.when(owner_z(ORDER[k]) == zh)
        def _():
            reduce_relay(early, ORDER[k])

    def relay(k):
        reduce_relay(late, ORDER[k])

    def slice_work(k):
        place = ORDER[k]
        dz, dy = place
        src = LS[place]
        down_load(k).wait()

        def step(b, _):
            used = sum((rank[b] * BLOCK < widths[g]).astype(jnp.int32) for g in range(LEVELS))
            level = jnp.maximum(used - 1, 0)
            l0, l1 = src[0, level], src[1, level]
            at = rows(b * BLOCK, BLOCK)
            h = hT[at, :]
            D[dz, dy, at, 0:256] = dot(h, l0).astype(BF16)
            D[dz, dy, at, 256:512] = dot(h, l1).astype(BF16)
            part = dot_nt(l0, wdb[k % 2, at, 0:256]) + dot_nt(l1, wdb[k % 2, at, 256:512])
            lane = cols(b * BLOCK, BLOCK)
            HG[:, lane] = part if k == 0 else HG[:, lane] + part
            return 0

        lax.fori_loop(0, nb, step, 0)
        if k + 2 < len(ORDER):
            down_load(k + 2).start()
        if k < 7:
            reduce_first(late, place)

    def row_loads(n, slot):
        core = jnp.where(n < 8, 1 - c, c)
        at = rows((2 * lax.rem(n, 8) + core) * 256, 256)
        return (
            pltpu.make_async_copy(wg.at[at, :], wrow.at[slot, :, cols(0, units)], ls.at[16 + 2 * slot]),
            pltpu.make_async_copy(wu.at[at, :], wrow.at[slot, :, cols(units, units)], ls.at[17 + 2 * slot]),
        )

    def input_part(first):
        def step(n, _):
            slot = lax.rem(n, 2)
            for cp in row_loads(n, slot):
                cp.wait()
            X[:, cols(n * 256, 256)] = dot_nt(G[0:tok, :], wrow[slot]).astype(BF16)

            @pl.when(n + 2 < 16)
            def _():
                for cp in row_loads(n + 2, slot):
                    cp.start()
            return 0

        lax.fori_loop(first, first + 4, step, 0)

    gl.neighbours0_late()
    gl.along_z()
    gl.got("C", (0, 0))
    slice_work(0)
    xt_along_z()
    gl.got("C", (1, 0))
    slice_work(1)
    gl.neighbours0()
    gl.got("C", (0, 3))
    slice_work(2)
    gl.got("C", (0, 1))
    slice_work(3)
    gl.opposite0_late()
    for k in range(4):
        early_send(k)
    relay(0)
    gl.opposite0()
    gl.neighbours1()
    gl.got("C", (0, 2))
    slice_work(4)
    early_send(4)
    xt_around_y()
    relay(1)
    gl.got("C", (1, 3))
    slice_work(5)
    early_send(5)
    gl.opposite1()
    gl.got("C", (1, 1))
    slice_work(6)
    early_send(6)
    relay(2)
    relay(3)
    for slot in range(2):
        for cp in row_loads(slot, slot):
            cp.start()
    gl.got("C", (1, 2))
    slice_work(7)
    early_send(7)

    def grads(b, _):
        at = cols(b * BLOCK, BLOCK)
        hg = HG[:, at]
        G[0:tok, at] = (hg * A[:, at]).astype(BF16)
        G[0:tok, cols(units + b * BLOCK, BLOCK)] = (hg * B[:, at]).astype(BF16)
        return 0

    lax.fori_loop(0, nb, grads, 0)

    from_m, from_p, far = {}, {}, {}

    def g_own(j):
        at = cols(j * 256, 256)
        src = G.at[pl.ds(0, tok), at]
        from_m[j] = send(src, G.at[pl.ds(3 * tok, tok), at], Xp)
        from_p[j] = send(src, G.at[pl.ds(tok, tok), at], Xm)

    def g_forward(j):
        at = cols(j * 256, 256)
        from_m[j].wait_recv()
        far[j, 0] = send(G.at[pl.ds(3 * tok, half_t), at], G.at[pl.ds(2 * tok, half_t), at], Xp)
        from_p[j].wait_recv()
        far[j, 1] = send(G.at[pl.ds(tok + half_t, half_t), at],
                         G.at[pl.ds(2 * tok + half_t, half_t), at], Xm)

    p_sent = {}

    def p_other(j):
        far[j, 0].wait_recv()
        far[j, 1].wait_recv()
        at = cols(j * 256, 256)
        for h in range(2):
            Ps[j, pl.ds(256 * h, 256), :] = dot(XT[1 - zh, pl.ds(256 * h, 256), :], G[:, at]).astype(BF16)
        p_sent[j] = send(Ps.at[j], Pr.at[j], Z2)

    def p_own(j):
        p_sent[j].wait_recv()
        at = cols(j * 256, 256)
        for h in range(2):
            r = pl.ds(256 * h, 256)
            out = (dot(XT[zh, r, :], G[:, at]) + Pr[j, r, :].astype(F32)).astype(BF16)
            for i in range(2):
                lane = j * 256 + i * BLOCK
                target, lane = (o_g, lane) if lane < units else (o_u, lane - units)
                target[r, lane:lane + BLOCK] = out[:, i * BLOCK:(i + 1) * BLOCK]
        for i in range(2):
            lane = j * 256 + i * BLOCK
            held, out, lane = (o_g, to_g, lane) if lane < units else (o_u, to_u, lane - units)
            store(held.at[:, cols(lane, BLOCK)], out.at[:, cols(lane, BLOCK)])

    def sum_x(part, zz):
        base, half, one, two, send1, recv1, send2, recv2 = part
        for side in range(2):
            for i in range(2):
                pltpu.make_async_remote_copy(
                    src_ref=D.at[0, 0, pl.ds(base, half)],
                    dst_ref=at_owner(two, part, zz, side, pl.ds(0, half)),
                    send_sem=at_owner(send2, part, zz, side, i), recv_sem=at_owner(recv2, part, zz, side, i),
                    device_id=Xp, device_id_type=MESH).wait_recv()

    def down_place(zz):
        return zl + zz - 2 * zl * zz, lax.rem(x - y + 4, 4)

    down_z = []

    def down_away():
        zz = 1 - zh
        sum_x(late, zz)
        dz, dy = down_place(zz)
        at = pl.ds(z_rows, units - z_rows)
        D[dz, dy, at, :] = (D[dz, dy, at, :].astype(F32) + R2[zz, 0].astype(F32)
                            + R2[zz, 1].astype(F32)).astype(BF16)
        down_z.append(send(D.at[dz, dy, at], R3.at[...], Z2))

    def down_own_early():
        if not z_rows:
            return
        sum_x(early, zh)
        dz, dy = down_place(zh)
        at = pl.ds(0, z_rows)
        o_d[at, :] = (D[dz, dy, at, :].astype(F32) + R2A[0].astype(F32) + R2A[1].astype(F32)).astype(BF16)
        store(o_d.at[at], to_d.at[at])

    def down_own():
        sum_x(late, zh)
        for cp in down_z:
            cp.wait_recv()
        dz, dy = down_place(zh)
        at = pl.ds(z_rows, units - z_rows)
        o_d[at, :] = (D[dz, dy, at, :].astype(F32) + R2[zh, 0].astype(F32) + R2[zh, 1].astype(F32)
                      + R3[...].astype(F32)).astype(BF16)
        store(o_d.at[at], to_d.at[at])

    in_y, in_z = [], []

    def input_sum_cores():
        in_c.wait_recv()
        for i in range(8):
            at = cols(2048 + 256 * i, 256)
            X[:, at] = (X[:, at].astype(F32) + IrC[:, cols(256 * i, 256)].astype(F32)).astype(BF16)
        for k, dev in ((1, Yp), (3, Ym), (2, Y2)):
            for zz in range(2):
                src = X.at[:, cols(2048 + zz * 1024 + lax.rem(y + k, 4) * 256, 256)]
                in_y.append(send(src, IrY.at[k - 1, zz], dev))

    def input_sum_y():
        for cp in in_y:
            cp.wait_recv()
        for zz in range(2):
            at = cols(2048 + zz * 1024 + y * 256, 256)
            total = X[:, at].astype(F32)
            for k in range(3):
                total = total + IrY[k, zz].astype(F32)
            X[:, at] = total.astype(BF16)
        in_z.append(send(X.at[:, cols(2048 + (1 - zl) * 1024 + y * 256, 256)], IrZ.at[...], Z1))

    def input_sum_z():
        in_z[0].wait_recv()
        o_in[...] = (X[:, cols(2048 + zl * 1024 + y * 256, 256)].astype(F32) + IrZ[...].astype(F32)).astype(BF16)
        store(o_in, to_in)

    g_own(0)
    g_own(1)
    reduce_first(late, ORDER[7])
    for cp in x_sends:
        cp.wait_send()
    input_part(0)
    relay(4)
    relay(5)
    g_forward(0)
    g_own(2)
    input_part(4)
    in_c = send(X.at[:, cols(0, 2048)], IrC.at[...], C)
    xt_cores()
    relay(6)
    g_forward(1)
    g_own(3)
    early_first(0)
    early_first(1)
    input_part(8)
    xt_moves["C"].wait_recv()
    p_other(0)
    g_forward(2)
    g_own(4)
    input_part(12)
    p_other(1)
    input_sum_cores()
    relay(7)
    early_first(2)
    early_first(3)
    early_relay(0)
    early_relay(1)
    g_forward(3)
    g_own(5)
    p_other(2)
    early_first(4)
    early_first(5)
    early_first(6)
    early_first(7)
    early_relay(2)
    early_relay(3)
    g_forward(4)
    g_own(6)
    p_other(3)
    input_sum_y()
    p_own(0)
    early_relay(4)
    early_relay(5)
    early_relay(6)
    early_relay(7)
    g_forward(5)
    down_away()
    p_other(4)
    p_own(1)
    g_forward(6)
    p_other(5)
    p_own(2)
    p_other(6)
    p_own(3)
    p_own(4)
    down_own_early()
    p_own(5)
    input_sum_z()
    down_own()
    p_own(6)

    assert len(started) <= COPIES and len(stored) <= 24
    for cp in stored:
        cp.wait()
    for cp in started:
        if not any(cp is other for other in x_sends):
            cp.wait_send()
    for place in ORDER:
        reduce_drain(late, place)
        if not z_rows:
            continue

        @pl.when(owner_z(place) == zh)
        def _():
            reduce_drain(early, place)

        @pl.when(owner_z(place) != zh)
        def _():
            z_copy(place).wait_send()


def hand_out(*refs):
    src, dst, held, sems = refs[:4], refs[4:8], refs[8:12], refs[12]
    into = [pltpu.make_async_copy(src[i], held[i], sems.at[0, i]) for i in range(4)]
    out = [pltpu.make_async_copy(held[i], dst[i], sems.at[1, i]) for i in range(4)]
    for cp in into:
        cp.start()
    for i in range(4):
        into[i].wait()
        out[i].start()
    for cp in out:
        cp.wait()


def on_device(inputs, w_gate, w_up, w_down, cotangents, prefix_widths, block_rank):
    tok = inputs.shape[0]
    width, units = w_gate.shape
    anywhere = pl.BlockSpec(memory_space=pl.ANY)
    smem = pl.BlockSpec(memory_space=pltpu.SMEM)
    share = width // 8
    z_rows = Z_BLOCKS * BLOCK
    held = max(z_rows, 32)
    V = pltpu.VMEM
    dma = pltpu.SemaphoreType.DMA
    scratch = [V((2, LEVELS, tok, 256), BF16) for _ in ORDER] + [
        V((tok, width), BF16),
        V((4, width // 2, 256), BF16),
        V((2, units, 512), BF16),
        V((2, 256, 2 * units), BF16),
        V((3, 64, tok), BF16),
        V((2, 512, 4 * tok), BF16),
        V((4 * tok, 2 * units), BF16),
        V((2, 4, units, 512), BF16),
        V((2, 2, (units - z_rows) // 2, 512), BF16),
        V((2, 2, units - z_rows, 512), BF16),
        V((units - z_rows, 512), BF16),
        V((7, 512, 256), BF16),
        V((7, 512, 256), BF16),
        V((tok, width // 2), BF16),
        V((tok, 256), BF16),
        V((3, 2, tok, 256), BF16),
        V((tok, units), F32),
        V((tok, units), F32),
        V((tok, units), F32),
        V((units, tok), BF16),
        dma((COPIES,)),
        dma((COPIES,)),
        dma((24,)),
        dma((2, 2)),
        dma((2, 2)),
        dma((2, 2, 2)),
        dma((2, 2, 2)),
        V((4, held, 512), BF16),
        V((2, held // 2, 512), BF16),
        V((2, held, 512), BF16),
        dma((2,)),
        dma((2,)),
        dma((2, 2)),
        dma((2, 2)),
        dma((4,)),
        dma((4,)),
        V((tok, 256), BF16),
        V((share, units), BF16),
        V((share, units), BF16),
        V((units, share), BF16),
        dma((24,)),
    ]
    results = pl.pallas_call(
        functools.partial(body, tok, width, units, z_rows),
        out_shape=(
            jax.ShapeDtypeStruct((tok, 256), BF16),
            jax.ShapeDtypeStruct((share, units), BF16),
            jax.ShapeDtypeStruct((share, units), BF16),
            jax.ShapeDtypeStruct((units, share), BF16),
        ),
        in_specs=[smem, smem] + [anywhere] * 5,
        out_specs=(anywhere,) * 4,
        scratch_shapes=scratch,
        compiler_params=pltpu.CompilerParams(
            collective_id=0, has_side_effects=True, vmem_limit_bytes=64 * 2**20),
        name="swiglu_backward",
    )(prefix_widths, block_rank, inputs, w_gate, w_up, w_down, cotangents)
    return pl.pallas_call(
        hand_out,
        out_shape=tuple(jax.ShapeDtypeStruct(r.shape, r.dtype) for r in results),
        in_specs=[anywhere] * 4,
        out_specs=(anywhere,) * 4,
        scratch_shapes=[V(r.shape, r.dtype) for r in results] + [dma((2, 4))],
        name="hand_out",
    )(*results)


def solution(mesh):
    placed = (
        P("seq", "tensor"),
        P(None, "tensor"),
        P(None, "tensor"),
        P("tensor", None),
        P(None, "seq", "tensor"),
        P(),
        P("tensor"),
    )
    return jax.shard_map(
        on_device,
        mesh=mesh,
        in_specs=placed,
        out_specs=(P("seq", "tensor"), P("seq", "tensor"), P("seq", "tensor"), P("tensor", "seq")),
        check_vma=False,
    )
```

```python
import functools

import jax
import jax.numpy as jnp
from jax import lax
from jax.experimental import pallas as pl
from jax.experimental.pallas import tpu as pltpu
from jax.sharding import PartitionSpec as P

BLOCK = 128
LEVELS = 4
MESH = pl.DeviceIdType.MESH
COPIES = 128
Z_BLOCKS = 4
F32 = jnp.float32
BF16 = jnp.bfloat16
NT = (((1,), (1,)), ((), ()))
ORDER = ((0, 0), (1, 0), (0, 3), (0, 1), (0, 2), (1, 3), (1, 1), (1, 2))


def dot(a, b):
    return jnp.dot(a, b, preferred_element_type=F32)


def dot_nt(a, b):
    return lax.dot_general(a, b, NT, preferred_element_type=F32)


def cols(start, size):
    return pl.ds(pl.multiple_of(start, 128), size)


def rows(start, size):
    return pl.ds(pl.multiple_of(start, 16), size)


def body(tok, width, units, z_rows, *refs):
    widths, rank, xin, wg, wu, wd, cot, to_in, to_g, to_u, to_d = refs[:11]
    (X, wt, wdb, wrow, XTs, XT, G, D, R1, R2, R3, Ps, Pr, IrC, IrZ, IrY, A, B, HG, hT,
     ss, rs, ls, s1, r1, s2, r2, RZ, R1A, R2A, s1a, r1a, s2a, r2a, sz, rz,
     o_in, o_g, o_u, o_d, so) = refs[11 + 8:]
    LS = {place: refs[11 + i] for i, place in enumerate(ORDER)}
    nb = units // BLOCK
    half_t, quarter = tok // 2, tok // 4
    nchunk = 2 * units // 256

    s, t = lax.axis_index("seq"), lax.axis_index("tensor")
    x, zh = lax.rem(s, 4), s // 4
    zl, y, c = t // 8, lax.rem(t // 2, 4), lax.rem(t, 2)
    at_x = lambda k: (zh * 4 + lax.rem(x + k, 4), t)
    at_y = lambda k: (s, zl * 8 + lax.rem(y + k, 4) * 2 + c)
    C = (s, t + 1 - 2 * c)
    Z1 = (s, t + 8 - 16 * zl)
    Z2 = ((1 - zh) * 4 + x, t)
    Xp, Xm, X2, Yp, Ym, Y2 = at_x(1), at_x(3), at_x(2), at_y(1), at_y(3), at_y(2)

    started = []
    local = []

    def send(src, dst, dev):
        i = len(started)
        cp = pltpu.make_async_remote_copy(
            src_ref=src, dst_ref=dst, send_sem=ss.at[i], recv_sem=rs.at[i],
            device_id=dev, device_id_type=MESH)
        cp.start()
        started.append(cp)
        return cp

    def load(src, dst):
        i = len(local)
        cp = pltpu.make_async_copy(src, dst, ls.at[i])
        cp.start()
        local.append(cp)
        return cp

    cot_loads = [load(cot.at[g], A.at[:, cols(256 * g, 256)]) for g in range(3)]
    cot_loads.append(load(cot.at[3], B.at[:, cols(0, 256)]))
    own_x = load(xin, X.at[:, cols(t * 256, 256)])

    half_w = width // 2

    def tile_half(n):
        h = n // nb
        return zl + h - 2 * zl * h

    stored = []

    def store(held, out):
        cp = pltpu.make_async_copy(held, out, so.at[len(stored)])
        cp.start()
        stored.append(cp)

    def tile_loads(n, slot):
        at, lane = rows(tile_half(n) * half_w, half_w), cols(lax.rem(n, nb) * BLOCK, BLOCK)
        return (
            pltpu.make_async_copy(wg.at[at, lane], wt.at[slot, :, cols(0, BLOCK)], ls.at[8 + 2 * slot]),
            pltpu.make_async_copy(wu.at[at, lane], wt.at[slot, :, cols(BLOCK, BLOCK)], ls.at[9 + 2 * slot]),
        )

    for slot in range(4):
        for cp in tile_loads(slot, slot):
            cp.start()

    def feature_slice(place):
        return (zl + place[0] - 2 * zl * place[0]) * 4 + lax.rem(y + place[1], 4)

    def down_load(k):
        return pltpu.make_async_copy(wd.at[:, cols(feature_slice(ORDER[k]) * 512, 512)],
                                     wdb.at[k % 2], ls.at[20 + k % 2])

    down_load(0).start()
    down_load(1).start()

    barrier = pltpu.get_barrier_semaphore()
    peers = (C, Z1, Z2, Xp, Xm, X2, Yp, Ym, Y2)
    for dev in peers:
        pl.semaphore_signal(barrier, inc=1, device_id=dev, device_id_type=MESH)
    pl.semaphore_wait(barrier, len(peers))

    def x_view(place, first, count):
        tt = feature_slice(place) * 2 + c
        return X.at[pl.ds(first * quarter, count * quarter), cols(tt * 256, 256)]

    def x_pair(place, moved, first, count):
        return x_view(place, first, count), x_view(place, first, count)

    def ls_pair(place, moved, first, count):
        levels = pl.ds(first, count)
        return LS[place].at[c, levels], LS[moved].at[c, levels]

    class Gather:
        def __init__(self, pair, cut):
            self.pair = pair
            self.cut = cut
            self.moves = {}

        def send(self, step, place, first=0, count=4, src=None):
            dz, dy = place
            moved, dev = {"C": (place, C), "Z": ((1 - dz, dy), Z1), "P": ((dz, (dy + 3) % 4), Yp),
                          "M": ((dz, (dy + 1) % 4), Ym)}[step[0]]
            mine, there = self.pair(place, moved, first, count)
            self.moves[step, place] = send(mine if src is None else src, there, dev)

        def got(self, step, place):
            self.moves[step, place].wait_recv()

        def late_z(self, place):
            if self.cut < 4:
                self.send("Z", place, self.cut, 4 - self.cut)

        def got_late_z(self, place):
            if self.cut < 4:
                self.got("Z", place)

        def along_z(self):
            self.got("Z", (0, 0))
            self.send("P", (1, 0), 0, self.cut)
            self.send("M", (1, 0), 0, self.cut)
            self.send("C", (1, 0))

        def neighbours0_late(self):
            self.got("P2", (0, 0))
            self.late_z((0, 3))
            self.got("M2", (0, 0))
            self.send("M", (0, 1), 2, 2)
            self.late_z((0, 1))

        def neighbours0(self):
            self.got("P", (0, 0))
            self.send("P", (0, 3), 0, 2)
            self.send("C", (0, 3))
            self.got("M", (0, 0))
            if self.cut == 4:
                self.send("M", (0, 1), 2, 2)
            self.send("C", (0, 1))

        def opposite0_late(self):
            self.got("M", (0, 1))
            self.late_z((0, 2))

        def opposite0(self):
            self.got("P", (0, 3))
            if self.cut == 4:
                self.got("M", (0, 1))
            self.send("C", (0, 2))

        def neighbours1(self):
            self.got("P", (1, 0))
            self.send("P", (1, 3), 0, self.cut // 2)
            self.got("M", (1, 0))
            self.send("M", (1, 1), self.cut // 2, self.cut // 2)
            self.got_late_z((0, 3))
            self.send("C", (1, 3))
            self.got_late_z((0, 1))
            self.send("C", (1, 1))

        def opposite1(self):
            self.got("P", (1, 3))
            self.got("M", (1, 1))
            self.got_late_z((0, 2))
            self.send("C", (1, 2))

    gx, gl = Gather(x_pair, 4), Gather(ls_pair, 2)
    for step in "ZPMC":
        gx.send(step, (0, 0), src=xin)

    for cp in cot_loads:
        cp.wait()
    total = A[:, 0:256]
    own = LS[(0, 0)]
    own[c, 0] = total.astype(BF16)
    for g in range(1, LEVELS):
        total = total + (A[:, 256 * g:256 * g + 256] if g < 3 else B[:, 0:256])
        own[c, g] = total.astype(BF16)

    gx.along_z()
    gl.send("Z", (0, 0))
    gl.send("C", (0, 0))
    gx.neighbours0()
    gx.opposite0()
    gx.neighbours1()
    gl.send("P2", (0, 0), 2, 2)
    gl.send("M2", (0, 0), 2, 2)
    gl.send("P", (0, 0), 0, 2)
    gl.send("M", (0, 0), 0, 2)
    own_x.wait()
    for dy in range(4):
        gx.got("C", (0, dy))

    def forward_part(n):
        slot = lax.rem(n, 4)
        for cp in tile_loads(n, slot):
            cp.wait()
        return dot(X[:, cols(tile_half(n) * half_w, half_w)], wt[slot])

    def tile_next(n):
        @pl.when(n + 4 < 2 * nb)
        def _():
            for cp in tile_loads(n + 4, lax.rem(n, 4)):
                cp.start()

    def forward_first(b, _):
        both = forward_part(b)
        tile_next(b)
        at = cols(b * BLOCK, BLOCK)
        A[:, at] = both[:, :BLOCK]
        B[:, at] = both[:, BLOCK:]
        return 0

    def forward(b, _):
        both = forward_part(b + nb)
        tile_next(b + nb)
        at = cols(b * BLOCK, BLOCK)
        gate, up = both[:, :BLOCK] + A[:, at], both[:, BLOCK:] + B[:, at]
        sigma = jax.nn.sigmoid(gate)
        active = gate * sigma
        A[:, at] = up * sigma * (1.0 + gate * (1.0 - sigma))
        B[:, at] = active
        hT[rows(b * BLOCK, BLOCK), :] = jnp.transpose((active * up).astype(BF16))
        return 0

    lax.fori_loop(0, nb, forward_first, 0)
    gx.opposite1()
    for dy in range(4):
        gx.got("C", (1, dy))
    x_sends = list(gx.moves.values())

    def transposed(zz):
        return jnp.transpose(X[:, cols((zz * 4 + x) * 512, 512)])

    share = 512 // 8
    mine = rows((zl * 4 + y) * share, share)
    far_tokens = pl.ds(tok, 3 * tok)
    x_moves = []
    for k, dev in ((1, Xp), (3, Xm), (2, X2)):
        lanes = cols((c * 4 + lax.rem(x + k, 4)) * 512 + (zl * 2 + y // 2) * 128, 128)
        block = jnp.transpose(X[:, lanes])
        XTs[k - 1] = jnp.where(lax.rem(y, 2) == 0, block[:share], block[share:])
        x_moves.append(send(XTs.at[k - 1], XT.at[c, mine, cols((4 - k) * tok, tok)], dev))
    for zz in range(2):
        XT[zz, :, 0:tok] = transposed(zz)
    xt_moves = {}

    def xt_along_z():
        for cp in x_moves:
            cp.wait_recv()
        piece = XT.at[c, mine, far_tokens]
        xt_moves["Z"] = send(piece, piece, Z1)

    def xt_around_y():
        xt_moves["Z"].wait_recv()
        for k, dev in ((1, Yp), (3, Ym), (2, Y2)):
            for h in range(2):
                piece = XT.at[c, rows((h * 4 + y) * share, share), far_tokens]
                xt_moves[k, h] = send(piece, piece, dev)

    def xt_cores():
        for k in (1, 3, 2):
            for h in range(2):
                xt_moves[k, h].wait_recv()
        piece = XT.at[c, :, far_tokens]
        xt_moves["C"] = send(piece, piece, C)

    lax.fori_loop(0, nb, forward, 0)

    def relation(place):
        return lax.rem(y + place[1] - x + 4, 4)

    def owner_z(place):
        return zl + place[0] - 2 * zl * place[0]

    early = (0, z_rows // 2, R1A, R2A, s1a, r1a, s2a, r2a)
    late = (z_rows, (units - z_rows) // 2, R1, R2, s1, r1, s2, r2)

    def at_owner(ref, part, zz, *index):
        return ref.at[index] if part is early else ref.at[(zz, *index)]

    def reduce_copy(part, place, kind):
        base, half, one, two, send1, recv1, send2, recv2 = part
        dz, dy = place
        zz = owner_z(place)
        if kind < 2:
            return pltpu.make_async_remote_copy(
                src_ref=D.at[dz, dy, pl.ds(base + kind * half, half)],
                dst_ref=at_owner(one, part, zz, kind),
                send_sem=at_owner(send1, part, zz, kind), recv_sem=at_owner(recv1, part, zz, kind),
                device_id=Xp if kind == 0 else Xm, device_id_type=MESH)
        rel = relation(place)
        side = rel // 2
        h = 1 - side if kind == 2 else side
        return pltpu.make_async_remote_copy(
            src_ref=D.at[dz, dy, rows(base + h * half, half)],
            dst_ref=at_owner(two, part, zz, side, rows(h * half, half)),
            send_sem=at_owner(send2, part, zz, side, kind - 2),
            recv_sem=at_owner(recv2, part, zz, side, kind - 2),
            device_id=at_x(rel), device_id_type=MESH)

    def reduce_first(part, place):
        rel = relation(place)

        @pl.when(rel == 2)
        def _():
            reduce_copy(part, place, 0).start()
            reduce_copy(part, place, 1).start()

        @pl.when(lax.rem(rel, 2) == 1)
        def _():
            reduce_copy(part, place, 2).start()

    def reduce_relay(part, place):
        base, half, one, two, send1, recv1, send2, recv2 = part
        dz, dy = place
        rel = relation(place)
        zz = owner_z(place)
        side = rel // 2

        @pl.when(lax.rem(rel, 2) == 1)
        def _():
            pltpu.make_async_remote_copy(
                src_ref=D.at[dz, dy, pl.ds(base, half)], dst_ref=at_owner(one, part, zz, side),
                send_sem=at_owner(send1, part, zz, side), recv_sem=at_owner(recv1, part, zz, side),
                device_id=Xp, device_id_type=MESH).wait_recv()
            span = rows(base + side * half, half)
            D[dz, dy, span, :] = (D[dz, dy, span, :].astype(F32)
                                  + at_owner(one, part, zz, side)[...].astype(F32)).astype(BF16)
            reduce_copy(part, place, 3).start()

    def reduce_drain(part, place):
        rel = relation(place)

        @pl.when(rel == 2)
        def _():
            reduce_copy(part, place, 0).wait_send()
            reduce_copy(part, place, 1).wait_send()

        @pl.when(lax.rem(rel, 2) == 1)
        def _():
            reduce_copy(part, place, 2).wait_send()
            reduce_copy(part, place, 3).wait_send()

    def z_copy(place):
        dz, dy = place
        return pltpu.make_async_remote_copy(
            src_ref=D.at[dz, dy, pl.ds(0, z_rows)], dst_ref=RZ.at[dy],
            send_sem=sz.at[dy], recv_sem=rz.at[dy], device_id=Z2, device_id_type=MESH)

    def early_send(k):
        if not z_rows:
            return

        @pl.when(owner_z(ORDER[k]) != zh)
        def _():
            z_copy(ORDER[k]).start()

    def early_first(k):
        if not z_rows:
            return
        place = ORDER[k]
        dz, dy = place

        @pl.when(owner_z(place) == zh)
        def _():
            z_copy(place).wait_recv()
            span = pl.ds(0, z_rows)
            D[dz, dy, span, :] = (D[dz, dy, span, :].astype(F32) + RZ[dy].astype(F32)).astype(BF16)
            reduce_first(early, place)

    def early_relay(k):
        if not z_rows:
            return
        @pl.when(owner_z(ORDER[k]) == zh)
        def _():
            reduce_relay(early, ORDER[k])

    def relay(k):
        reduce_relay(late, ORDER[k])

    def slice_work(k):
        place = ORDER[k]
        dz, dy = place
        src = LS[place]
        down_load(k).wait()

        def step(b, _):
            used = sum((rank[b] * BLOCK < widths[g]).astype(jnp.int32) for g in range(LEVELS))
            level = jnp.maximum(used - 1, 0)
            l0, l1 = src[0, level], src[1, level]
            at = rows(b * BLOCK, BLOCK)
            h = hT[at, :]
            D[dz, dy, at, 0:256] = dot(h, l0).astype(BF16)
            D[dz, dy, at, 256:512] = dot(h, l1).astype(BF16)
            part = dot_nt(l0, wdb[k % 2, at, 0:256]) + dot_nt(l1, wdb[k % 2, at, 256:512])
            lane = cols(b * BLOCK, BLOCK)
            HG[:, lane] = part if k == 0 else HG[:, lane] + part
            return 0

        lax.fori_loop(0, nb, step, 0)
        if k + 2 < len(ORDER):
            down_load(k + 2).start()
        if k < 7:
            reduce_first(late, place)

    def row_loads(n, slot):
        core = jnp.where(n < 8, 1 - c, c)
        at = rows((2 * lax.rem(n, 8) + core) * 256, 256)
        return (
            pltpu.make_async_copy(wg.at[at, :], wrow.at[slot, :, cols(0, units)], ls.at[16 + 2 * slot]),
            pltpu.make_async_copy(wu.at[at, :], wrow.at[slot, :, cols(units, units)], ls.at[17 + 2 * slot]),
        )

    def input_part(first):
        def step(n, _):
            slot = lax.rem(n, 2)
            for cp in row_loads(n, slot):
                cp.wait()
            X[:, cols(n * 256, 256)] = dot_nt(G[0:tok, :], wrow[slot]).astype(BF16)

            @pl.when(n + 2 < 16)
            def _():
                for cp in row_loads(n + 2, slot):
                    cp.start()
            return 0

        lax.fori_loop(first, first + 4, step, 0)

    gl.neighbours0_late()
    gl.along_z()
    gl.got("C", (0, 0))
    slice_work(0)
    xt_along_z()
    gl.got("C", (1, 0))
    slice_work(1)
    gl.neighbours0()
    gl.got("C", (0, 3))
    slice_work(2)
    gl.got("C", (0, 1))
    slice_work(3)
    gl.opposite0_late()
    for k in range(4):
        early_send(k)
    relay(0)
    gl.opposite0()
    gl.neighbours1()
    gl.got("C", (0, 2))
    slice_work(4)
    early_send(4)
    xt_around_y()
    relay(1)
    gl.got("C", (1, 3))
    slice_work(5)
    early_send(5)
    gl.opposite1()
    gl.got("C", (1, 1))
    slice_work(6)
    early_send(6)
    relay(2)
    relay(3)
    for slot in range(2):
        for cp in row_loads(slot, slot):
            cp.start()
    gl.got("C", (1, 2))
    slice_work(7)
    early_send(7)

    def grads(b, _):
        at = cols(b * BLOCK, BLOCK)
        hg = HG[:, at]
        G[0:tok, at] = (hg * A[:, at]).astype(BF16)
        G[0:tok, cols(units + b * BLOCK, BLOCK)] = (hg * B[:, at]).astype(BF16)
        return 0

    lax.fori_loop(0, nb, grads, 0)

    from_m, from_p, far = {}, {}, {}

    def g_own(j):
        at = cols(j * 256, 256)
        src = G.at[pl.ds(0, tok), at]
        from_m[j] = send(src, G.at[pl.ds(3 * tok, tok), at], Xp)
        from_p[j] = send(src, G.at[pl.ds(tok, tok), at], Xm)

    def g_forward(j):
        at = cols(j * 256, 256)
        from_m[j].wait_recv()
        far[j, 0] = send(G.at[pl.ds(3 * tok, half_t), at], G.at[pl.ds(2 * tok, half_t), at], Xp)
        from_p[j].wait_recv()
        far[j, 1] = send(G.at[pl.ds(tok + half_t, half_t), at],
                         G.at[pl.ds(2 * tok + half_t, half_t), at], Xm)

    p_sent = {}

    def p_other(j):
        far[j, 0].wait_recv()
        far[j, 1].wait_recv()
        at = cols(j * 256, 256)
        for h in range(2):
            Ps[j, pl.ds(256 * h, 256), :] = dot(XT[1 - zh, pl.ds(256 * h, 256), :], G[:, at]).astype(BF16)
        p_sent[j] = send(Ps.at[j], Pr.at[j], Z2)

    def p_own(j):
        p_sent[j].wait_recv()
        at = cols(j * 256, 256)
        for h in range(2):
            r = pl.ds(256 * h, 256)
            out = (dot(XT[zh, r, :], G[:, at]) + Pr[j, r, :].astype(F32)).astype(BF16)
            for i in range(2):
                lane = j * 256 + i * BLOCK
                target, lane = (o_g, lane) if lane < units else (o_u, lane - units)
                target[r, lane:lane + BLOCK] = out[:, i * BLOCK:(i + 1) * BLOCK]
        for i in range(2):
            lane = j * 256 + i * BLOCK
            held, out, lane = (o_g, to_g, lane) if lane < units else (o_u, to_u, lane - units)
            store(held.at[:, cols(lane, BLOCK)], out.at[:, cols(lane, BLOCK)])

    def sum_x(part, zz):
        base, half, one, two, send1, recv1, send2, recv2 = part
        for side in range(2):
            for i in range(2):
                pltpu.make_async_remote_copy(
                    src_ref=D.at[0, 0, pl.ds(base, half)],
                    dst_ref=at_owner(two, part, zz, side, pl.ds(0, half)),
                    send_sem=at_owner(send2, part, zz, side, i), recv_sem=at_owner(recv2, part, zz, side, i),
                    device_id=Xp, device_id_type=MESH).wait_recv()

    def down_place(zz):
        return zl + zz - 2 * zl * zz, lax.rem(x - y + 4, 4)

    down_z = []

    def down_away():
        zz = 1 - zh
        sum_x(late, zz)
        dz, dy = down_place(zz)
        at = pl.ds(z_rows, units - z_rows)
        D[dz, dy, at, :] = (D[dz, dy, at, :].astype(F32) + R2[zz, 0].astype(F32)
                            + R2[zz, 1].astype(F32)).astype(BF16)
        down_z.append(send(D.at[dz, dy, at], R3.at[...], Z2))

    def down_own_early():
        if not z_rows:
            return
        sum_x(early, zh)
        dz, dy = down_place(zh)
        at = pl.ds(0, z_rows)
        o_d[at, :] = (D[dz, dy, at, :].astype(F32) + R2A[0].astype(F32) + R2A[1].astype(F32)).astype(BF16)
        store(o_d.at[at], to_d.at[at])

    def down_own():
        sum_x(late, zh)
        for cp in down_z:
            cp.wait_recv()
        dz, dy = down_place(zh)
        at = pl.ds(z_rows, units - z_rows)
        o_d[at, :] = (D[dz, dy, at, :].astype(F32) + R2[zh, 0].astype(F32) + R2[zh, 1].astype(F32)
                      + R3[...].astype(F32)).astype(BF16)
        store(o_d.at[at], to_d.at[at])

    in_y, in_z = [], []

    def input_sum_cores():
        in_c.wait_recv()
        for i in range(8):
            at = cols(2048 + 256 * i, 256)
            X[:, at] = (X[:, at].astype(F32) + IrC[:, cols(256 * i, 256)].astype(F32)).astype(BF16)
        for k, dev in ((1, Yp), (3, Ym), (2, Y2)):
            for zz in range(2):
                src = X.at[:, cols(2048 + zz * 1024 + lax.rem(y + k, 4) * 256, 256)]
                in_y.append(send(src, IrY.at[k - 1, zz], dev))

    def input_sum_y():
        for cp in in_y:
            cp.wait_recv()
        for zz in range(2):
            at = cols(2048 + zz * 1024 + y * 256, 256)
            total = X[:, at].astype(F32)
            for k in range(3):
                total = total + IrY[k, zz].astype(F32)
            X[:, at] = total.astype(BF16)
        in_z.append(send(X.at[:, cols(2048 + (1 - zl) * 1024 + y * 256, 256)], IrZ.at[...], Z1))

    def input_sum_z():
        in_z[0].wait_recv()
        o_in[...] = (X[:, cols(2048 + zl * 1024 + y * 256, 256)].astype(F32) + IrZ[...].astype(F32)).astype(BF16)
        store(o_in, to_in)

    g_own(0)
    g_own(1)
    reduce_first(late, ORDER[7])
    for cp in x_sends:
        cp.wait_send()
    input_part(0)
    relay(4)
    relay(5)
    g_forward(0)
    g_own(2)
    input_part(4)
    in_c = send(X.at[:, cols(0, 2048)], IrC.at[...], C)
    xt_cores()
    relay(6)
    g_forward(1)
    g_own(3)
    early_first(0)
    early_first(1)
    input_part(8)
    xt_moves["C"].wait_recv()
    p_other(0)
    g_forward(2)
    g_own(4)
    input_part(12)
    p_other(1)
    input_sum_cores()
    relay(7)
    early_first(2)
    early_first(3)
    early_relay(0)
    early_relay(1)
    g_forward(3)
    g_own(5)
    p_other(2)
    early_first(4)
    early_first(5)
    early_first(6)
    early_first(7)
    early_relay(2)
    early_relay(3)
    g_forward(4)
    g_own(6)
    p_other(3)
    input_sum_y()
    p_own(0)
    early_relay(4)
    early_relay(5)
    early_relay(6)
    early_relay(7)
    g_forward(5)
    down_away()
    p_other(4)
    p_own(1)
    g_forward(6)
    p_other(5)
    p_own(2)
    p_other(6)
    p_own(3)
    p_own(4)
    down_own_early()
    p_own(5)
    input_sum_z()
    down_own()
    p_own(6)

    assert len(started) <= COPIES and len(stored) <= 24
    for cp in stored:
        cp.wait()
    for cp in started:
        if not any(cp is other for other in x_sends):
            cp.wait_send()
    for place in ORDER:
        reduce_drain(late, place)
        if not z_rows:
            continue

        @pl.when(owner_z(place) == zh)
        def _():
            reduce_drain(early, place)

        @pl.when(owner_z(place) != zh)
        def _():
            z_copy(place).wait_send()


def hand_out(*refs):
    src, dst, held, sems = refs[:4], refs[4:8], refs[8:12], refs[12]
    into, out = [], []
    for part in range(4):
        for i in range(4):
            size = src[i].shape[0] // 4
            at = pl.ds(part * size, size)
            into.append(pltpu.make_async_copy(src[i].at[at], held[i].at[at], sems.at[0, i, part]))
            out.append(pltpu.make_async_copy(held[i].at[at], dst[i].at[at], sems.at[1, i, part]))
    for cp in into:
        cp.start()
    for arrived, leaving in zip(into, out):
        arrived.wait()
        leaving.start()
    for cp in out:
        cp.wait()


def on_device(inputs, w_gate, w_up, w_down, cotangents, prefix_widths, block_rank):
    tok = inputs.shape[0]
    width, units = w_gate.shape
    anywhere = pl.BlockSpec(memory_space=pl.ANY)
    smem = pl.BlockSpec(memory_space=pltpu.SMEM)
    share = width // 8
    z_rows = Z_BLOCKS * BLOCK
    held = max(z_rows, 32)
    V = pltpu.VMEM
    dma = pltpu.SemaphoreType.DMA
    scratch = [V((2, LEVELS, tok, 256), BF16) for _ in ORDER] + [
        V((tok, width), BF16),
        V((4, width // 2, 256), BF16),
        V((2, units, 512), BF16),
        V((2, 256, 2 * units), BF16),
        V((3, 64, tok), BF16),
        V((2, 512, 4 * tok), BF16),
        V((4 * tok, 2 * units), BF16),
        V((2, 4, units, 512), BF16),
        V((2, 2, (units - z_rows) // 2, 512), BF16),
        V((2, 2, units - z_rows, 512), BF16),
        V((units - z_rows, 512), BF16),
        V((7, 512, 256), BF16),
        V((7, 512, 256), BF16),
        V((tok, width // 2), BF16),
        V((tok, 256), BF16),
        V((3, 2, tok, 256), BF16),
        V((tok, units), F32),
        V((tok, units), F32),
        V((tok, units), F32),
        V((units, tok), BF16),
        dma((COPIES,)),
        dma((COPIES,)),
        dma((24,)),
        dma((2, 2)),
        dma((2, 2)),
        dma((2, 2, 2)),
        dma((2, 2, 2)),
        V((4, held, 512), BF16),
        V((2, held // 2, 512), BF16),
        V((2, held, 512), BF16),
        dma((2,)),
        dma((2,)),
        dma((2, 2)),
        dma((2, 2)),
        dma((4,)),
        dma((4,)),
        V((tok, 256), BF16),
        V((share, units), BF16),
        V((share, units), BF16),
        V((units, share), BF16),
        dma((24,)),
    ]
    results = pl.pallas_call(
        functools.partial(body, tok, width, units, z_rows),
        out_shape=(
            jax.ShapeDtypeStruct((tok, 256), BF16),
            jax.ShapeDtypeStruct((share, units), BF16),
            jax.ShapeDtypeStruct((share, units), BF16),
            jax.ShapeDtypeStruct((units, share), BF16),
        ),
        in_specs=[smem, smem] + [anywhere] * 5,
        out_specs=(anywhere,) * 4,
        scratch_shapes=scratch,
        compiler_params=pltpu.CompilerParams(
            collective_id=0, has_side_effects=True, vmem_limit_bytes=64 * 2**20),
        name="swiglu_backward",
    )(prefix_widths, block_rank, inputs, w_gate, w_up, w_down, cotangents)
    return pl.pallas_call(
        hand_out,
        out_shape=tuple(jax.ShapeDtypeStruct(r.shape, r.dtype) for r in results),
        in_specs=[anywhere] * 4,
        out_specs=(anywhere,) * 4,
        scratch_shapes=[V(r.shape, r.dtype) for r in results] + [dma((2, 4, 4))],
        name="hand_out",
    )(*results)


def solution(mesh):
    placed = (
        P("seq", "tensor"),
        P(None, "tensor"),
        P(None, "tensor"),
        P("tensor", None),
        P(None, "seq", "tensor"),
        P(),
        P("tensor"),
    )
    return jax.shard_map(
        on_device,
        mesh=mesh,
        in_specs=placed,
        out_specs=(P("seq", "tensor"), P("seq", "tensor"), P("seq", "tensor"), P("tensor", "seq")),
        check_vma=False,
    )
```
